256 devices in a mesh: gx: 4 (over x), gy: 8 (over y, core), gz: 8 (over z).
Axes of the slice: x: 4, y: 4, z: 8, core: 2. Of those that a mesh axis runs over, the one named last changes fastest.
Arguments:
- field: bfloat16 [512, 512, 2048], P('gx', 'gy', 'gz'), may hold values from -64 to 64
- sketch: float32 [512, 128], replicated, may hold values from -6 to 6
Outputs:
- factor: float32 [512, 128], replicated
- core: bfloat16 [128, 512, 2048], P(('gx', 'gy'), None, 'gz')
The draws below stay inside these ranges and needn't reach their ends.
All inputs are finite; a program needn't handle non-finite values.
Results may differ from the reference program's by a relative error of at most 0.012.
Values may be sent and summed in bfloat16 or wider, within the bound.
A program may use at most 128 MiB of HBM per device.

```python
import math
import jax
import jax.numpy as jnp
from jax import lax

N1 = 512
N2 = 512
RANK = 128
ITERS = 2
COLS = 2048


def draw_field(key, part):
    key_noise, key_rows, key_rough = jax.random.split(key, 3)
    shape = (N1, N2, COLS)
    noise = jax.random.truncated_normal(key_noise, -5.0, 5.0, shape, jnp.float32)
    mixed = noise + 0.3 * jnp.roll(noise, 1, axis=0)
    region_gain = jnp.exp(jax.random.uniform(key_rows, (N1, 16, 1, 8, 1), jnp.float32, 0.0, math.log(4.0)))
    region_gain = jnp.broadcast_to(region_gain, (N1, 16, N2 // 16, 8, COLS // 8)).reshape(shape)
    along = jnp.arange(N2, dtype=jnp.float32).reshape(1, N2, 1) / (N2 - 1) - 0.5
    across = jnp.arange(COLS, dtype=jnp.float32).reshape(1, 1, COLS) / (COLS - 1) - 0.5
    rough = jax.random.uniform(key_rough, (1, N2, COLS), jnp.float32, -0.6, 0.6)
    col_scale = jnp.exp(math.log(8.0) * (along + across) + rough) * 0.25
    result = region_gain * mixed * col_scale
    return jnp.clip(result, -60.0, 60.0).astype(jnp.bfloat16)


def scatter_about(rng, extent, scale, reach, kind=jnp.bfloat16):
    return jnp.clip(scale * jax.random.normal(rng, extent, jnp.float32), -reach, reach).astype(kind)


def setup_inputs(seed: int = 0) -> dict:
    keys = jax.random.split(jax.random.key(seed), 3)
    field = draw_field(jax.random.fold_in(keys[2], 71), 0)
    sketch = scatter_about(keys[1], (N1, RANK), 1.0, 6.0, jnp.float32)
    return dict(field=field, sketch=sketch)


def orthonormal(gram, sketch):
    basis = sketch
    for sweep in range(ITERS):
        image = jnp.dot(gram, basis, precision=lax.Precision.HIGHEST)
        inner = jnp.dot(image.T, image, precision=lax.Precision.HIGHEST)
        lower = jnp.linalg.cholesky(inner)
        basis = jax.scipy.linalg.solve_triangular(lower, image.T, lower=True).T
    return basis

def reference(field, sketch):
    unfolded = field.reshape(N1, N2 * COLS)
    gram = lax.dot_general(unfolded.astype(jnp.float32), unfolded.astype(jnp.float32), (((1,), (1,)), ((), ())), preferred_element_type=jnp.float32)
    factor = orthonormal(gram, sketch)
    factor_low = factor.astype(jnp.bfloat16)
    core = lax.dot_general(factor_low.astype(jnp.float32), unfolded.astype(jnp.float32), (((0,), (0,)), ((), ())), preferred_element_type=jnp.float32)
    core = core.astype(jnp.bfloat16).reshape(RANK, N2, COLS)
    return (factor, core)
```

```python
import functools

import jax
import jax.numpy as jnp
from jax import lax
from jax.experimental import pallas as pl
from jax.experimental.pallas import tpu as pltpu
from jax.sharding import PartitionSpec as P

ITERS = 2
MESH = pl.DeviceIdType.MESH
GX, GY, GZ = 4, 8, 8
YC = GY // 2
PLANE = GX * YC
SUB = 4


def remote(src, dst, send, recv, dev):
    return pltpu.make_async_remote_copy(
        src_ref=src, dst_ref=dst, send_sem=send, recv_sem=recv,
        device_id=dev, device_id_type=MESH,
    )


def swap16():
    row = lax.broadcasted_iota(jnp.int32, (256, 256), 0)
    col = lax.broadcasted_iota(jnp.int32, (256, 256), 1)
    hit = ((row & 15) * 16 + (row >> 4)) == col
    return jnp.where(hit, 1.0, 0.0).astype(jnp.bfloat16)


def gram_kernel(field, xs, gfin, raw, perm, gp, r1, acc, r2, r3, a_send, a_recv, own_sem,
                c_send, c_recv, p_send, p_recv, z_send, z_recv, g_send, g_recv, f_send, f_recv):
    x, y, z = lax.axis_index("gx"), lax.axis_index("gy"), lax.axis_index("gz")
    core, yc = lax.rem(y, 2), lax.div(y, 2)
    other = (x, y + 1 - 2 * core, z)

    def xdev(d):
        return (lax.rem(x + d, GX), y, z)

    def zdev(d):
        return (x, y, lax.rem(z + d, GZ))

    def pdev(d):
        return (lax.rem(x + d // YC, GX), 2 * lax.rem(yc + d % YC, YC) + core, z)

    def pnum(d):
        return lax.rem(x + d // YC + GX, GX) * YC + lax.rem(yc + d % YC, YC)

    def pfrom(d):
        return lax.rem(x - d // YC + GX, GX) * YC + lax.rem(yc - d % YC + YC, YC)

    barrier = pltpu.get_barrier_semaphore()
    peers = [pdev(d) for d in range(1, PLANE)] + [zdev(d) for d in range(1, GZ)] + [other]
    for dev in peers:
        pl.semaphore_signal(barrier, inc=1, device_id=dev, device_id_type=MESH)

    rows = field.shape[0] // SUB
    pieces = 16
    mine = pltpu.make_async_copy(
        field.at[:, pl.ds(pl.multiple_of(x * pieces, pieces), pieces), :], raw.at[0], own_sem
    )
    mine.start()
    perm[...] = swap16()
    pl.semaphore_wait(barrier, len(peers))

    sends = {}
    for d in (1, 3, 2):
        to = lax.rem(x + d, GX)
        for s in range(SUB):
            sends[d, s] = remote(
                field.at[pl.ds(s * rows, rows), pl.ds(pl.multiple_of(to * pieces, pieces), pieces), :],
                raw.at[GX - d, pl.ds(s * rows, rows)],
                a_send.at[d * SUB + s], a_recv.at[(GX - d) * SUB + s], xdev(d),
            )
            sends[d, s].start()

    def relayout(d, s):
        base = pl.multiple_of(lax.rem(x + d, GX) * 128, 128)

        def group(g, carry):
            i0 = s * rows + g * 16
            block = raw[d, pl.ds(i0, 16)].reshape(256, 256)
            out = jnp.dot(perm[...], block, preferred_element_type=jnp.float32).astype(jnp.bfloat16)
            for j in range(16):
                xs[pl.ds(pl.multiple_of(base + i0, 16), 16), j * 256:(j + 1) * 256] = out[j * 16:(j + 1) * 16]
            return carry

        lax.fori_loop(0, rows // 16, group, 0)

    def block(a, b, pos):
        def part(k, total):
            k0 = pl.multiple_of(k * 1024, 1024)
            u = xs[pl.ds(pl.multiple_of(a * 128, 128), 128), pl.ds(k0, 1024)]
            v = xs[pl.ds(pl.multiple_of(b * 128, 128), 128), pl.ds(k0, 1024)]
            return total + lax.dot_general(u, v, (((1,), (1,)), ((), ())), preferred_element_type=jnp.float32)

        out = lax.fori_loop(0, 4, part, jnp.zeros((128, 128), jnp.float32))
        gp[pl.ds(pl.multiple_of(pos * 128, 128), 128), :] = out

    mine.wait()
    for s in range(SUB):
        relayout(0, s)
    m1, p1, p2 = lax.rem(x + 3, GX), lax.rem(x + 1, GX), lax.rem(x + 2, GX)
    block(x, x, x)
    for d in (1, 3):
        for s in range(SUB):
            sends[GX - d, s].wait_recv()
            relayout(d, s)
    block(p1, p1, p1)
    block(m1, m1, m1)
    block(x, p1, 4 + x)
    block(m1, x, 4 + m1)
    odd = lax.rem(x + 1, 2)
    block(odd, odd + 2, 8 + odd)
    for s in range(SUB):
        sends[2, s].wait_recv()
        relayout(2, s)
    block(p2, p2, p2)
    block(p1, p2, 4 + p1)
    block(p2, m1, 4 + p2)
    even = lax.rem(x, 2)
    block(even, even + 2, 8 + even)

    half = 640
    to_other = remote(gp.at[pl.ds(pl.multiple_of((1 - core) * half, half), half)], r1, c_send, c_recv, other)
    to_other.start()
    to_other.wait_recv()
    acc[...] = gp[pl.ds(pl.multiple_of(core * half, half), half)] + r1[...]

    piece = half // PLANE
    me = pnum(0)
    order = [10, 2, 8, 6, 9, 11, 14, 1, 3, 4, 12, 5, 7, 13, 15]
    plane = {}
    for d in order:
        plane[d] = remote(
            acc.at[pl.ds(pl.multiple_of(pnum(d) * piece, 8), piece)], r2.at[me],
            p_send.at[d], p_recv.at[d], pdev(d),
        )
        plane[d].start()
    r2[me] = acc[pl.ds(pl.multiple_of(me * piece, 8), piece)]
    for d in order:
        remote(r2.at[pfrom(d)], r2.at[pfrom(d)], p_send.at[d], p_recv.at[d], pdev(d)).wait_recv()
    total = r2[0]
    for q in range(1, PLANE):
        total = total + r2[q]
    r3[z] = total

    along = {}
    for d in (4, 3, 5, 2, 6, 1, 7):
        along[d] = remote(r3.at[z], r3.at[z], z_send.at[d], z_recv.at[d], zdev(d))
        along[d].start()
    for d in (1, 7, 2, 6, 3, 5, 4):
        src = lax.rem(z - d + GZ, GZ)
        remote(r3.at[src], r3.at[src], z_send.at[d], z_recv.at[d], zdev(d)).wait_recv()
    total = r3[0]
    for q in range(1, GZ):
        total = total + r3[q]

    def place(q):
        return gfin.at[pl.ds(pl.multiple_of(core * half + q * piece, 8), piece)]

    gfin[pl.ds(pl.multiple_of(core * half + me * piece, 8), piece)] = total
    spread = {}
    for d in order:
        spread[d] = remote(place(me), place(me), g_send.at[d], g_recv.at[d], pdev(d))
        spread[d].start()
    onward = {0: remote(place(me), place(me), f_send.at[0], f_recv.at[0], other)}
    onward[0].start()
    for d in order[::-1]:
        at = place(pfrom(d))
        remote(at, at, g_send.at[d], g_recv.at[d], pdev(d)).wait_recv()
        onward[d] = remote(at, at, f_send.at[d], f_recv.at[d], other)
        onward[d].start()
    for d in range(PLANE):
        there = gfin.at[pl.ds(pl.multiple_of((1 - core) * half + pfrom(d) * piece, 8), piece)]
        remote(there, there, f_send.at[d], f_recv.at[d], other).wait_recv()

    for copies in (sends, plane, along, spread, onward):
        for c in copies.values():
            c.wait_send()
    to_other.wait_send()


def core_kernel(factor_t, xs, out, perm, t, buf, send, recv, own_sem):
    x, y, z = lax.axis_index("gx"), lax.axis_index("gy"), lax.axis_index("gz")

    def dev(dx, dy):
        return (lax.rem(x + dx, GX), lax.rem(y + dy, GY), z)

    offsets = [(dx, dy) for dx in (2, 1, 3, 0) for dy in (4, 5, 3, 2, 6, 7, 1, 0)]
    barrier = pltpu.get_barrier_semaphore()
    for dx, dy in offsets[:-1]:
        pl.semaphore_signal(barrier, inc=1, device_id=dev(dx, dy), device_id_type=MESH)
    perm[...] = swap16()

    def product(j, carry):
        cols = pl.ds(pl.multiple_of(j * 256, 256), 256)
        t[:, cols] = jnp.dot(factor_t[...], xs[:, cols], preferred_element_type=jnp.float32).astype(jnp.bfloat16)
        return carry

    lax.fori_loop(0, 16, product, 0)
    pl.semaphore_wait(barrier, len(offsets) - 1)

    def place(px, py):
        return out.at[:, pl.ds(pl.multiple_of(py * 64 + px * 16, 16), 16), :]

    copies = {}
    for dx in (2, 1, 3, 0):
        to = lax.rem(x + dx, GX)

        def group(g, carry):
            r0 = pl.multiple_of(to * 32 + g * 16, 16)
            block = jnp.concatenate([t[pl.ds(r0, 16), j * 256:(j + 1) * 256] for j in range(16)], axis=0)
            rows = jnp.dot(perm[...], block, preferred_element_type=jnp.float32).astype(jnp.bfloat16)
            buf[pl.ds(r0, 16)] = rows.reshape(16, 16, 256)
            return carry

        lax.fori_loop(0, 2, group, 0)
        for k, dy in enumerate((4, 5, 3, 2, 6, 7, 1, 0)):
            src = buf.at[pl.ds(to * 32 + lax.rem(y + dy, GY) * 4, 4)]
            if dx or dy:
                n = dx * GY + dy
                copies[n] = remote(src, place(x, y), send.at[n], recv.at[n], dev(dx, dy))
                copies[n].start()
            else:
                mine = pltpu.make_async_copy(src, place(x, y), own_sem)
                mine.start()
    for dx, dy in offsets[:-1]:
        n = dx * GY + dy
        at = place(lax.rem(x - dx + GX, GX), lax.rem(y - dy + GY, GY))
        remote(at, at, send.at[n], recv.at[n], dev(dx, dy)).wait_recv()
    for c in copies.values():
        c.wait_send()
    mine.wait()


def orthonormal(gram, sketch):
    basis = sketch
    for sweep in range(ITERS):
        image = jnp.dot(gram, basis, precision=lax.Precision.HIGHEST)
        inner = jnp.dot(image.T, image, precision=lax.Precision.HIGHEST)
        lower = jnp.linalg.cholesky(inner)
        basis = jax.scipy.linalg.solve_triangular(lower, image.T, lower=True).T
    return basis


def assemble(packed):
    b = packed.reshape(10, 128, 128)
    grid = [[None] * 4 for _ in range(4)]
    for a in range(4):
        grid[a][a] = b[a]
        n = (a + 1) % 4
        grid[a][n], grid[n][a] = b[4 + a], b[4 + a].T
    for a in range(2):
        grid[a][a + 2], grid[a + 2][a] = b[8 + a], b[8 + a].T
    return jnp.block(grid)


VMEM = pl.BlockSpec(memory_space=pltpu.VMEM)
ANY = pl.BlockSpec(memory_space=pl.ANY)
DMA = pltpu.SemaphoreType.DMA


def shards(field, sketch):
    xs, packed = pl.pallas_call(
        gram_kernel,
        out_shape=(
            jax.ShapeDtypeStruct((512, 4096), jnp.bfloat16),
            jax.ShapeDtypeStruct((1280, 128), jnp.float32),
        ),
        in_specs=[ANY],
        out_specs=(VMEM, VMEM),
        scratch_shapes=[
            pltpu.VMEM((GX, 128, 16, 256), jnp.bfloat16),
            pltpu.VMEM((256, 256), jnp.bfloat16),
            pltpu.VMEM((1280, 128), jnp.float32),
            pltpu.VMEM((640, 128), jnp.float32),
            pltpu.VMEM((640, 128), jnp.float32),
            pltpu.VMEM((PLANE, 40, 128), jnp.float32),
            pltpu.VMEM((GZ, 40, 128), jnp.float32),
            DMA((GX * SUB,)), DMA((GX * SUB,)), DMA,
            DMA, DMA,
            DMA((PLANE,)), DMA((PLANE,)),
            DMA((GZ,)), DMA((GZ,)),
            DMA((PLANE,)), DMA((PLANE,)),
            DMA((PLANE,)), DMA((PLANE,)),
        ],
        compiler_params=pltpu.CompilerParams(
            collective_id=0, has_side_effects=True, vmem_limit_bytes=40 * 2**20
        ),
        name="gram",
    )(field)
    factor = orthonormal(assemble(packed), sketch)
    factor_t = factor.astype(jnp.bfloat16).T
    core = pl.pallas_call(
        core_kernel,
        out_shape=jax.ShapeDtypeStruct((4, 512, 256), jnp.bfloat16),
        in_specs=[VMEM, VMEM],
        out_specs=ANY,
        scratch_shapes=[
            pltpu.VMEM((256, 256), jnp.bfloat16),
            pltpu.VMEM((128, 4096), jnp.bfloat16),
            pltpu.VMEM((128, 16, 256), jnp.bfloat16),
            DMA((GX * GY,)), DMA((GX * GY,)), DMA,
        ],
        compiler_params=pltpu.CompilerParams(
            collective_id=1, has_side_effects=True, vmem_limit_bytes=40 * 2**20
        ),
        name="core",
    )(factor_t, xs)
    return (factor, core)


def solution(mesh):
    return jax.shard_map(
        shards,
        mesh=mesh,
        in_specs=(P("gx", "gy", "gz"), P()),
        out_specs=(P(), P(("gx", "gy"), None, "gz")),
        check_vma=False,
    )
```

```python
import functools

import jax
import jax.numpy as jnp
from jax import lax
from jax.experimental import pallas as pl
from jax.experimental.pallas import tpu as pltpu
from jax.sharding import PartitionSpec as P

ITERS = 2
MESH = pl.DeviceIdType.MESH
GX, GY, GZ = 4, 8, 8
YC = GY // 2
PLANE = GX * YC
SUB = 4


def remote(src, dst, send, recv, dev):
    return pltpu.make_async_remote_copy(
        src_ref=src, dst_ref=dst, send_sem=send, recv_sem=recv,
        device_id=dev, device_id_type=MESH,
    )


def swap16():
    row = lax.broadcasted_iota(jnp.int32, (256, 256), 0)
    col = lax.broadcasted_iota(jnp.int32, (256, 256), 1)
    hit = ((row & 15) * 16 + (row >> 4)) == col
    return jnp.where(hit, 1.0, 0.0).astype(jnp.bfloat16)


def gram_kernel(field, xs_out, gfin, raw, xs, out_sem, perm, gp, r1, acc, r2, r3, a_send, a_recv, own_sem,
                c_send, c_recv, p_send, p_recv, z_send, z_recv, g_send, g_recv, f_send, f_recv):
    x, y, z = lax.axis_index("gx"), lax.axis_index("gy"), lax.axis_index("gz")
    core, yc = lax.rem(y, 2), lax.div(y, 2)
    other = (x, y + 1 - 2 * core, z)

    def xdev(d):
        return (lax.rem(x + d, GX), y, z)

    def zdev(d):
        return (x, y, lax.rem(z + d, GZ))

    def pdev(d):
        return (lax.rem(x + d // YC, GX), 2 * lax.rem(yc + d % YC, YC) + core, z)

    def pnum(d):
        return lax.rem(x + d // YC + GX, GX) * YC + lax.rem(yc + d % YC, YC)

    def pfrom(d):
        return lax.rem(x - d // YC + GX, GX) * YC + lax.rem(yc - d % YC + YC, YC)

    barrier = pltpu.get_barrier_semaphore()
    peers = [pdev(d) for d in range(1, PLANE)] + [zdev(d) for d in range(1, GZ)] + [other]
    for dev in peers:
        pl.semaphore_signal(barrier, inc=1, device_id=dev, device_id_type=MESH)

    rows = field.shape[0] // SUB
    pieces = 16
    mine = pltpu.make_async_copy(
        field.at[:, pl.ds(pl.multiple_of(x * pieces, pieces), pieces), :], raw.at[0], own_sem
    )
    mine.start()
    perm[...] = swap16()
    pl.semaphore_wait(barrier, len(peers))

    sends = {}
    for d in (1, 3, 2):
        to = lax.rem(x + d, GX)
        for s in range(SUB):
            sends[d, s] = remote(
                field.at[pl.ds(s * rows, rows), pl.ds(pl.multiple_of(to * pieces, pieces), pieces), :],
                raw.at[GX - d, pl.ds(s * rows, rows)],
                a_send.at[d * SUB + s], a_recv.at[(GX - d) * SUB + s], xdev(d),
            )
            sends[d, s].start()

    def relayout(d, s):
        base = pl.multiple_of(lax.rem(x + d, GX) * 128, 128)

        def group(g, carry):
            i0 = s * rows + g * 16
            block = raw[d, pl.ds(i0, 16)].reshape(256, 256)
            out = jnp.dot(perm[...], block, preferred_element_type=jnp.float32).astype(jnp.bfloat16)
            for j in range(16):
                xs[pl.ds(pl.multiple_of(base + i0, 16), 16), j * 256:(j + 1) * 256] = out[j * 16:(j + 1) * 16]
            return carry

        lax.fori_loop(0, rows // 16, group, 0)

    def keep(d):
        rows_of = pl.ds(pl.multiple_of(lax.rem(x + d, GX) * 128, 128), 128)
        out = pltpu.make_async_copy(xs.at[rows_of], xs_out.at[rows_of], out_sem.at[d])
        out.start()
        return out

    def block(a, b, pos):
        def part(k, total):
            k0 = pl.multiple_of(k * 1024, 1024)
            u = xs[pl.ds(pl.multiple_of(a * 128, 128), 128), pl.ds(k0, 1024)]
            v = xs[pl.ds(pl.multiple_of(b * 128, 128), 128), pl.ds(k0, 1024)]
            return total + lax.dot_general(u, v, (((1,), (1,)), ((), ())), preferred_element_type=jnp.float32)

        out = lax.fori_loop(0, 4, part, jnp.zeros((128, 128), jnp.float32))
        gp[pl.ds(pl.multiple_of(pos * 128, 128), 128), :] = out

    mine.wait()
    for s in range(SUB):
        relayout(0, s)
    kept = [keep(0)]
    m1, p1, p2 = lax.rem(x + 3, GX), lax.rem(x + 1, GX), lax.rem(x + 2, GX)
    block(x, x, x)
    for d in (1, 3):
        for s in range(SUB):
            sends[GX - d, s].wait_recv()
            relayout(d, s)
        kept.append(keep(d))
    block(p1, p1, p1)
    block(m1, m1, m1)
    block(x, p1, 4 + x)
    block(m1, x, 4 + m1)
    odd = lax.rem(x + 1, 2)
    block(odd, odd + 2, 8 + odd)
    for s in range(SUB):
        sends[2, s].wait_recv()
        relayout(2, s)
    kept.append(keep(2))
    block(p2, p2, p2)
    block(p1, p2, 4 + p1)
    block(p2, m1, 4 + p2)
    even = lax.rem(x, 2)
    block(even, even + 2, 8 + even)

    half = 640
    to_other = remote(gp.at[pl.ds(pl.multiple_of((1 - core) * half, half), half)], r1, c_send, c_recv, other)
    to_other.start()
    to_other.wait_recv()
    acc[...] = gp[pl.ds(pl.multiple_of(core * half, half), half)] + r1[...]

    piece = half // PLANE
    me = pnum(0)
    order = [10, 2, 8, 6, 9, 11, 14, 1, 3, 4, 12, 5, 7, 13, 15]
    plane = {}
    for d in order:
        plane[d] = remote(
            acc.at[pl.ds(pl.multiple_of(pnum(d) * piece, 8), piece)], r2.at[me],
            p_send.at[d], p_recv.at[d], pdev(d),
        )
        plane[d].start()
    r2[me] = acc[pl.ds(pl.multiple_of(me * piece, 8), piece)]
    for d in order:
        remote(r2.at[pfrom(d)], r2.at[pfrom(d)], p_send.at[d], p_recv.at[d], pdev(d)).wait_recv()
    total = r2[0]
    for q in range(1, PLANE):
        total = total + r2[q]
    r3[z] = total

    along = {}
    for d in (4, 3, 5, 2, 6, 1, 7):
        along[d] = remote(r3.at[z], r3.at[z], z_send.at[d], z_recv.at[d], zdev(d))
        along[d].start()
    for d in (1, 7, 2, 6, 3, 5, 4):
        src = lax.rem(z - d + GZ, GZ)
        remote(r3.at[src], r3.at[src], z_send.at[d], z_recv.at[d], zdev(d)).wait_recv()
    total = r3[0]
    for q in range(1, GZ):
        total = total + r3[q]

    def place(q):
        return gfin.at[pl.ds(pl.multiple_of(core * half + q * piece, 8), piece)]

    gfin[pl.ds(pl.multiple_of(core * half + me * piece, 8), piece)] = total
    spread = {}
    for d in order:
        spread[d] = remote(place(me), place(me), g_send.at[d], g_recv.at[d], pdev(d))
        spread[d].start()
    onward = {0: remote(place(me), place(me), f_send.at[0], f_recv.at[0], other)}
    onward[0].start()
    for d in order[::-1]:
        at = place(pfrom(d))
        remote(at, at, g_send.at[d], g_recv.at[d], pdev(d)).wait_recv()
        onward[d] = remote(at, at, f_send.at[d], f_recv.at[d], other)
        onward[d].start()
    for d in range(PLANE):
        there = gfin.at[pl.ds(pl.multiple_of((1 - core) * half + pfrom(d) * piece, 8), piece)]
        remote(there, there, f_send.at[d], f_recv.at[d], other).wait_recv()

    for copies in (sends, plane, along, spread, onward):
        for c in copies.values():
            c.wait_send()
    to_other.wait_send()
    for c in kept:
        c.wait()


def core_kernel(factor_t, xs_in, out, xs, in_sem, perm, t, buf, send, recv, own_sem):
    x, y, z = lax.axis_index("gx"), lax.axis_index("gy"), lax.axis_index("gz")

    def dev(dx, dy):
        return (lax.rem(x + dx, GX), lax.rem(y + dy, GY), z)

    offsets = [(dx, dy) for dx in (2, 1, 3, 0) for dy in (4, 5, 3, 2, 6, 7, 1, 0)]
    barrier = pltpu.get_barrier_semaphore()
    for dx, dy in offsets[:-1]:
        pl.semaphore_signal(barrier, inc=1, device_id=dev(dx, dy), device_id_type=MESH)
    loads = []
    for k in range(4):
        cols = slice(k * 1024, (k + 1) * 1024)
        loads.append(pltpu.make_async_copy(xs_in.at[:, cols], xs.at[:, cols], in_sem.at[k]))
        loads[k].start()
    perm[...] = swap16()

    def product(j, carry):
        cols = pl.ds(pl.multiple_of(j * 256, 256), 256)
        t[:, cols] = jnp.dot(factor_t[...], xs[:, cols], preferred_element_type=jnp.float32).astype(jnp.bfloat16)
        return carry

    for k in range(4):
        loads[k].wait()
        lax.fori_loop(4 * k, 4 * k + 4, product, 0)
    pl.semaphore_wait(barrier, len(offsets) - 1)

    def place(px, py):
        return out.at[:, pl.ds(pl.multiple_of(py * 64 + px * 16, 16), 16), :]

    copies = {}
    for dx in (2, 1, 3, 0):
        to = lax.rem(x + dx, GX)

        def group(g, carry):
            r0 = pl.multiple_of(to * 32 + g * 16, 16)
            block = jnp.concatenate([t[pl.ds(r0, 16), j * 256:(j + 1) * 256] for j in range(16)], axis=0)
            rows = jnp.dot(perm[...], block, preferred_element_type=jnp.float32).astype(jnp.bfloat16)
            buf[pl.ds(r0, 16)] = rows.reshape(16, 16, 256)
            return carry

        lax.fori_loop(0, 2, group, 0)
        for k, dy in enumerate((4, 5, 3, 2, 6, 7, 1, 0)):
            src = buf.at[pl.ds(to * 32 + lax.rem(y + dy, GY) * 4, 4)]
            if dx or dy:
                n = dx * GY + dy
                copies[n] = remote(src, place(x, y), send.at[n], recv.at[n], dev(dx, dy))
                copies[n].start()
            else:
                mine = pltpu.make_async_copy(src, place(x, y), own_sem)
                mine.start()
    for dx, dy in offsets[:-1]:
        n = dx * GY + dy
        at = place(lax.rem(x - dx + GX, GX), lax.rem(y - dy + GY, GY))
        remote(at, at, send.at[n], recv.at[n], dev(dx, dy)).wait_recv()
    for c in copies.values():
        c.wait_send()
    mine.wait()


def split3(q):
    a = q.astype(jnp.bfloat16).astype(jnp.float32)
    b = (q - a).astype(jnp.bfloat16).astype(jnp.float32)
    return a, b, q - a - b


def eliminate(a, d, base):
    lane = lax.broadcasted_iota(jnp.int32, (8, 128), 1)
    sub = lax.broadcasted_iota(jnp.int32, (8, 128), 0)
    inside = (lane >= base) & (lane < base + 8)
    rows = [jnp.broadcast_to(a[base + i:base + i + 1, :], (8, 128)) for i in range(8)]
    s = [[jnp.broadcast_to(rows[i][:, base + k:base + k + 1], (8, 128)) for k in range(i + 1)] for i in range(8)]
    w = [jnp.where(inside, jnp.where(lane == base + i, 1.0, 0.0), rows[i]) for i in range(8)]
    inverse = []
    for k in range(8):
        inverse.append(1.0 / s[k][k])
        for i in range(k + 1, 8):
            m = s[i][k] * inverse[k]
            for l in range(k + 1, i + 1):
                s[i][l] = s[i][l] - m * s[l][k]
            w[i] = w[i] - m * w[k]
    p, scale, pivot = w[0], inverse[0], s[0][0]
    for i in range(1, 8):
        p = jnp.where(sub == i, w[i], p)
        scale = jnp.where(sub == i, inverse[i], scale)
        pivot = jnp.where(sub == i, s[i][i], pivot)
    d[base:base + 8, :] = pivot
    return p, p * scale, inside


def inverse_cholesky(a, d):
    for base in range(0, 128, 8):
        p, scaled, inside = eliminate(a, d, base)
        a[base:base + 8, :] = p
        after = base + 8
        if after < 128:
            u, v = split3(p), split3(scaled)
            left = jnp.concatenate([u[0], u[0], u[1], u[0], u[1], u[2]], axis=0)
            right = jnp.concatenate([v[0], v[1], v[0], v[2], v[1], v[0]], axis=0).astype(jnp.bfloat16)
            change = jnp.dot(left.T.astype(jnp.bfloat16), right, preferred_element_type=jnp.float32)
            old = a[after:, :]
            a[after:, :] = jnp.where(jnp.broadcast_to(inside[:1], old.shape), 0.0, old) - change[after:, :]


def exact_dot(u, v, dims=((1,), (0,))):
    return lax.dot_general(u, v, (dims, ((), ())), precision=lax.Precision.HIGHEST, preferred_element_type=jnp.float32)


def factor_kernel(packed, sketch, factor, factor_t, gram, basis, image, a, d):
    def block(k):
        return packed[128 * k:128 * k + 128, :]

    def put(i, j, value):
        gram[128 * i:128 * i + 128, 128 * j:128 * j + 128] = value

    for k in range(4):
        put(k, k, block(k))
        n = (k + 1) % 4
        put(k, n, block(4 + k))
        put(n, k, block(4 + k).T)
    for k in range(2):
        put(k, k + 2, block(8 + k))
        put(k + 2, k, block(8 + k).T)
    basis[...] = sketch[...].T

    def sweep(step, carry):
        image[...] = exact_dot(basis[...], gram[...])
        a[...] = exact_dot(image[...], image[...], ((1,), (1,)))
        inverse_cholesky(a, d)
        row = lax.broadcasted_iota(jnp.int32, (128, 128), 0)
        col = lax.broadcasted_iota(jnp.int32, (128, 128), 1)
        lower = jnp.where(col <= row, a[...] * lax.rsqrt(d[...]), 0.0)
        basis[...] = exact_dot(lower, image[...])
        return carry

    lax.fori_loop(0, ITERS, sweep, 0)
    factor_t[...] = basis[...].astype(jnp.bfloat16)
    factor[...] = basis[...].T


VMEM = pl.BlockSpec(memory_space=pltpu.VMEM)
ANY = pl.BlockSpec(memory_space=pl.ANY)
DMA = pltpu.SemaphoreType.DMA


def shards(field, sketch):
    xs, packed = pl.pallas_call(
        gram_kernel,
        out_shape=(
            jax.ShapeDtypeStruct((512, 4096), jnp.bfloat16),
            jax.ShapeDtypeStruct((1280, 128), jnp.float32),
        ),
        in_specs=[ANY],
        out_specs=(ANY, VMEM),
        scratch_shapes=[
            pltpu.VMEM((GX, 128, 16, 256), jnp.bfloat16),
            pltpu.VMEM((512, 4096), jnp.bfloat16),
            DMA((GX,)),
            pltpu.VMEM((256, 256), jnp.bfloat16),
            pltpu.VMEM((1280, 128), jnp.float32),
            pltpu.VMEM((640, 128), jnp.float32),
            pltpu.VMEM((640, 128), jnp.float32),
            pltpu.VMEM((PLANE, 40, 128), jnp.float32),
            pltpu.VMEM((GZ, 40, 128), jnp.float32),
            DMA((GX * SUB,)), DMA((GX * SUB,)), DMA,
            DMA, DMA,
            DMA((PLANE,)), DMA((PLANE,)),
            DMA((GZ,)), DMA((GZ,)),
            DMA((PLANE,)), DMA((PLANE,)),
            DMA((PLANE,)), DMA((PLANE,)),
        ],
        compiler_params=pltpu.CompilerParams(
            collective_id=0, has_side_effects=True, vmem_limit_bytes=60 * 2**20
        ),
        name="gram",
    )(field)
    factor, factor_t = pl.pallas_call(
        factor_kernel,
        out_shape=(
            jax.ShapeDtypeStruct((512, 128), jnp.float32),
            jax.ShapeDtypeStruct((128, 512), jnp.bfloat16),
        ),
        in_specs=[VMEM, VMEM],
        out_specs=(VMEM, VMEM),
        scratch_shapes=[
            pltpu.VMEM((512, 512), jnp.float32),
            pltpu.VMEM((128, 512), jnp.float32),
            pltpu.VMEM((128, 512), jnp.float32),
            pltpu.VMEM((128, 128), jnp.float32),
            pltpu.VMEM((128, 128), jnp.float32),
        ],
        compiler_params=pltpu.CompilerParams(vmem_limit_bytes=60 * 2**20),
        name="factor",
    )(packed, sketch)
    core = pl.pallas_call(
        core_kernel,
        out_shape=jax.ShapeDtypeStruct((4, 512, 256), jnp.bfloat16),
        in_specs=[VMEM, ANY],
        out_specs=ANY,
        scratch_shapes=[
            pltpu.VMEM((512, 4096), jnp.bfloat16),
            DMA((4,)),
            pltpu.VMEM((256, 256), jnp.bfloat16),
            pltpu.VMEM((128, 4096), jnp.bfloat16),
            pltpu.VMEM((128, 16, 256), jnp.bfloat16),
            DMA((GX * GY,)), DMA((GX * GY,)), DMA,
        ],
        compiler_params=pltpu.CompilerParams(
            collective_id=1, has_side_effects=True, vmem_limit_bytes=60 * 2**20
        ),
        name="core",
    )(factor_t, xs)
    return (factor, core)


def solution(mesh):
    return jax.shard_map(
        shards,
        mesh=mesh,
        in_specs=(P("gx", "gy", "gz"), P()),
        out_specs=(P(), P(("gx", "gy"), None, "gz")),
        check_vma=False,
    )
```

```python
import functools

import jax
import jax.numpy as jnp
from jax import lax
from jax.experimental import pallas as pl
from jax.experimental.pallas import tpu as pltpu
from jax.sharding import PartitionSpec as P

ITERS = 2
MESH = pl.DeviceIdType.MESH
GX, GY, GZ = 4, 8, 8
YC = GY // 2
PLANE = GX * YC
SUB = 4


def remote(src, dst, send, recv, dev):
    return pltpu.make_async_remote_copy(
        src_ref=src, dst_ref=dst, send_sem=send, recv_sem=recv,
        device_id=dev, device_id_type=MESH,
    )


def swap16():
    row = lax.broadcasted_iota(jnp.int32, (256, 256), 0)
    col = lax.broadcasted_iota(jnp.int32, (256, 256), 1)
    hit = ((row & 15) * 16 + (row >> 4)) == col
    return jnp.where(hit, 1.0, 0.0).astype(jnp.bfloat16)


def gram_kernel(field, xs, gfin, raw, perm, gp, r1, acc, r2, r3, a_send, a_recv, own_sem,
                c_send, c_recv, p_send, p_recv, z_send, z_recv, g_send, g_recv, f_send, f_recv):
    x, y, z = lax.axis_index("gx"), lax.axis_index("gy"), lax.axis_index("gz")
    core, yc = lax.rem(y, 2), lax.div(y, 2)
    other = (x, y + 1 - 2 * core, z)

    def xdev(d):
        return (lax.rem(x + d, GX), y, z)

    def zdev(d):
        return (x, y, lax.rem(z + d, GZ))

    def pdev(d):
        return (lax.rem(x + d // YC, GX), 2 * lax.rem(yc + d % YC, YC) + core, z)

    def pnum(d):
        return lax.rem(x + d // YC + GX, GX) * YC + lax.rem(yc + d % YC, YC)

    def pfrom(d):
        return lax.rem(x - d // YC + GX, GX) * YC + lax.rem(yc - d % YC + YC, YC)

    barrier = pltpu.get_barrier_semaphore()
    peers = [pdev(d) for d in range(1, PLANE)] + [zdev(d) for d in range(1, GZ)] + [other]
    for dev in peers:
        pl.semaphore_signal(barrier, inc=1, device_id=dev, device_id_type=MESH)

    rows = field.shape[0] // SUB
    pieces = 16
    mine = pltpu.make_async_copy(
        field.at[:, pl.ds(pl.multiple_of(x * pieces, pieces), pieces), :], raw.at[0], own_sem
    )
    mine.start()
    perm[...] = swap16()
    pl.semaphore_wait(barrier, len(peers))

    sends = {}
    for d in (1, 3, 2):
        to = lax.rem(x + d, GX)
        for s in range(SUB):
            sends[d, s] = remote(
                field.at[pl.ds(s * rows, rows), pl.ds(pl.multiple_of(to * pieces, pieces), pieces), :],
                raw.at[GX - d, pl.ds(s * rows, rows)],
                a_send.at[d * SUB + s], a_recv.at[(GX - d) * SUB + s], xdev(d),
            )
            sends[d, s].start()

    def relayout(d, s):
        base = pl.multiple_of(lax.rem(x + d, GX) * 128, 128)

        def group(g, carry):
            i0 = s * rows + g * 16
            block = raw[d, pl.ds(i0, 16)].reshape(256, 256)
            out = jnp.dot(perm[...], block, preferred_element_type=jnp.float32).astype(jnp.bfloat16)
            for j in range(16):
                xs[pl.ds(pl.multiple_of(base + i0, 16), 16), j * 256:(j + 1) * 256] = out[j * 16:(j + 1) * 16]
            return carry

        lax.fori_loop(0, rows // 16, group, 0)

    def block(a, b, pos):
        def part(k, total):
            k0 = pl.multiple_of(k * 1024, 1024)
            u = xs[pl.ds(pl.multiple_of(a * 128, 128), 128), pl.ds(k0, 1024)]
            v = xs[pl.ds(pl.multiple_of(b * 128, 128), 128), pl.ds(k0, 1024)]
            return total + lax.dot_general(u, v, (((1,), (1,)), ((), ())), preferred_element_type=jnp.float32)

        out = lax.fori_loop(0, 4, part, jnp.zeros((128, 128), jnp.float32))
        gp[pl.ds(pl.multiple_of(pos * 128, 128), 128), :] = out

    mine.wait()
    for s in range(SUB):
        relayout(0, s)
    m1, p1, p2 = lax.rem(x + 3, GX), lax.rem(x + 1, GX), lax.rem(x + 2, GX)
    block(x, x, x)
    for d in (1, 3):
        for s in range(SUB):
            sends[GX - d, s].wait_recv()
            relayout(d, s)
    block(p1, p1, p1)
    block(m1, m1, m1)
    block(x, p1, 4 + x)
    block(m1, x, 4 + m1)
    odd = lax.rem(x + 1, 2)
    block(odd, odd + 2, 8 + odd)
    for s in range(SUB):
        sends[2, s].wait_recv()
        relayout(2, s)
    block(p2, p2, p2)
    block(p1, p2, 4 + p1)
    block(p2, m1, 4 + p2)
    even = lax.rem(x, 2)
    block(even, even + 2, 8 + even)

    half = 640
    to_other = remote(gp.at[pl.ds(pl.multiple_of((1 - core) * half, half), half)], r1, c_send, c_recv, other)
    to_other.start()
    to_other.wait_recv()
    acc[...] = gp[pl.ds(pl.multiple_of(core * half, half), half)] + r1[...]

    piece = half // PLANE
    me = pnum(0)
    order = [10, 2, 8, 6, 9, 11, 14, 1, 3, 4, 12, 5, 7, 13, 15]
    plane = {}
    for d in order:
        plane[d] = remote(
            acc.at[pl.ds(pl.multiple_of(pnum(d) * piece, 8), piece)], r2.at[me],
            p_send.at[d], p_recv.at[d], pdev(d),
        )
        plane[d].start()
    r2[me] = acc[pl.ds(pl.multiple_of(me * piece, 8), piece)]
    for d in order:
        remote(r2.at[pfrom(d)], r2.at[pfrom(d)], p_send.at[d], p_recv.at[d], pdev(d)).wait_recv()
    total = r2[0]
    for q in range(1, PLANE):
        total = total + r2[q]
    r3[z] = total

    along = {}
    for d in (4, 3, 5, 2, 6, 1, 7):
        along[d] = remote(r3.at[z], r3.at[z], z_send.at[d], z_recv.at[d], zdev(d))
        along[d].start()
    for d in (1, 7, 2, 6, 3, 5, 4):
        src = lax.rem(z - d + GZ, GZ)
        remote(r3.at[src], r3.at[src], z_send.at[d], z_recv.at[d], zdev(d)).wait_recv()
    total = r3[0]
    for q in range(1, GZ):
        total = total + r3[q]

    def place(q):
        return gfin.at[pl.ds(pl.multiple_of(core * half + q * piece, 8), piece)]

    gfin[pl.ds(pl.multiple_of(core * half + me * piece, 8), piece)] = total
    spread = {}
    for d in order:
        spread[d] = remote(place(me), place(me), g_send.at[d], g_recv.at[d], pdev(d))
        spread[d].start()
    onward = {0: remote(place(me), place(me), f_send.at[0], f_recv.at[0], other)}
    onward[0].start()
    for d in order[::-1]:
        at = place(pfrom(d))
        remote(at, at, g_send.at[d], g_recv.at[d], pdev(d)).wait_recv()
        onward[d] = remote(at, at, f_send.at[d], f_recv.at[d], other)
        onward[d].start()
    for d in range(PLANE):
        there = gfin.at[pl.ds(pl.multiple_of((1 - core) * half + pfrom(d) * piece, 8), piece)]
        remote(there, there, f_send.at[d], f_recv.at[d], other).wait_recv()

    for copies in (sends, plane, along, spread, onward):
        for c in copies.values():
            c.wait_send()
    to_other.wait_send()


def core_kernel(factor_t, xs, out, perm, t, buf, send, recv, own_sem):
    x, y, z = lax.axis_index("gx"), lax.axis_index("gy"), lax.axis_index("gz")

    def dev(dx, dy):
        return (lax.rem(x + dx, GX), lax.rem(y + dy, GY), z)

    offsets = [(dx, dy) for dx in (2, 1, 3, 0) for dy in (4, 5, 3, 2, 6, 7, 1, 0)]
    barrier = pltpu.get_barrier_semaphore()
    for dx, dy in offsets[:-1]:
        pl.semaphore_signal(barrier, inc=1, device_id=dev(dx, dy), device_id_type=MESH)
    perm[...] = swap16()

    def product(j, carry):
        cols = pl.ds(pl.multiple_of(j * 256, 256), 256)
        t[:, cols] = jnp.dot(factor_t[...], xs[:, cols], preferred_element_type=jnp.float32).astype(jnp.bfloat16)
        return carry

    lax.fori_loop(0, 16, product, 0)
    pl.semaphore_wait(barrier, len(offsets) - 1)

    def place(px, py):
        return out.at[:, pl.ds(pl.multiple_of(py * 64 + px * 16, 16), 16), :]

    copies = {}
    for dx in (2, 1, 3, 0):
        to = lax.rem(x + dx, GX)

        def group(g, carry):
            r0 = pl.multiple_of(to * 32 + g * 16, 16)
            block = jnp.concatenate([t[pl.ds(r0, 16), j * 256:(j + 1) * 256] for j in range(16)], axis=0)
            rows = jnp.dot(perm[...], block, preferred_element_type=jnp.float32).astype(jnp.bfloat16)
            buf[pl.ds(r0, 16)] = rows.reshape(16, 16, 256)
            return carry

        lax.fori_loop(0, 2, group, 0)
        for k, dy in enumerate((4, 5, 3, 2, 6, 7, 1, 0)):
            src = buf.at[pl.ds(to * 32 + lax.rem(y + dy, GY) * 4, 4)]
            if dx or dy:
                n = dx * GY + dy
                copies[n] = remote(src, place(x, y), send.at[n], recv.at[n], dev(dx, dy))
                copies[n].start()
            else:
                mine = pltpu.make_async_copy(src, place(x, y), own_sem)
                mine.start()
    for dx, dy in offsets[:-1]:
        n = dx * GY + dy
        at = place(lax.rem(x - dx + GX, GX), lax.rem(y - dy + GY, GY))
        remote(at, at, send.at[n], recv.at[n], dev(dx, dy)).wait_recv()
    for c in copies.values():
        c.wait_send()
    mine.wait()


def split3(q):
    a = q.astype(jnp.bfloat16).astype(jnp.float32)
    b = (q - a).astype(jnp.bfloat16).astype(jnp.float32)
    return a, b, q - a - b


def total_of(terms):
    while len(terms) > 1:
        terms = [terms[i] + terms[i + 1] if i + 1 < len(terms) else terms[i] for i in range(0, len(terms), 2)]
    return terms[0]


def inverse_cholesky(a, d):
    lane = lax.broadcasted_iota(jnp.int32, (8, 128), 1)
    sub = lax.broadcasted_iota(jnp.int32, (8, 128), 0)

    def repeat(v, l):
        return jnp.broadcast_to(v[:, l:l + 1], (8, 128))

    rows = [jnp.broadcast_to(a[i:i + 1, :], (8, 128)) for i in range(8)]
    for base in range(0, 128, 8):
        inside = (lane >= base) & (lane < base + 8)
        s = [[repeat(rows[i], base + k) for k in range(i + 1)] for i in range(8)]
        w = [jnp.where(inside, jnp.where(lane == base + i, 1.0, 0.0), rows[i]) for i in range(8)]
        inverse = []
        for k in range(8):
            inverse.append(1.0 / s[k][k])
            for i in range(k + 1, 8):
                m = s[i][k] * inverse[k]
                for l in range(k + 1, i + 1):
                    s[i][l] = s[i][l] - m * s[l][k]
                w[i] = w[i] - m * w[k]
        p, scale, pivot = w[0], inverse[0], s[0][0]
        for i in range(1, 8):
            p = jnp.where(sub == i, w[i], p)
            scale = jnp.where(sub == i, inverse[i], scale)
            pivot = jnp.where(sub == i, s[i][i], pivot)
        a[base:base + 8, :] = p
        d[base:base + 8, :] = pivot
        now, after = base + 8, base + 16
        if now < 128:
            before = [jnp.broadcast_to(a[now + i:now + i + 1, :], (8, 128)) for i in range(8)]
            rows = [
                jnp.where(inside, 0.0, before[i])
                - total_of([repeat(w[k], now + i) * inverse[k] * w[k] for k in range(8)])
                for i in range(8)
            ]
        if after < 128:
            u, v = split3(p), split3(p * scale)
            left = jnp.concatenate([u[0], u[0], u[1], u[0], u[1], u[2]], axis=0).astype(jnp.bfloat16)
            right = jnp.concatenate([v[0], v[1], v[0], v[2], v[1], v[0]], axis=0).astype(jnp.bfloat16)
            change = lax.dot_general(left, right, (((0,), (0,)), ((), ())), preferred_element_type=jnp.float32)
            old = a[after:, :]
            a[after:, :] = jnp.where(jnp.broadcast_to(inside[:1], old.shape), 0.0, old) - change[after:, :]


def exact_dot(u, v, dims=((1,), (0,))):
    return lax.dot_general(u, v, (dims, ((), ())), precision=lax.Precision.HIGHEST, preferred_element_type=jnp.float32)


def factor_kernel(packed, sketch, factor, factor_t, gram, basis, image, a, d, diagonal):
    def block(k):
        return packed[128 * k:128 * k + 128, :]

    def put(i, j, value):
        gram[128 * i:128 * i + 128, 128 * j:128 * j + 128] = value

    for k in range(4):
        put(k, k, block(k))
        n = (k + 1) % 4
        put(k, n, block(4 + k))
        put(n, k, block(4 + k).T)
    for k in range(2):
        put(k, k + 2, block(8 + k))
        put(k + 2, k, block(8 + k).T)
    start = sketch[...].T
    row = lax.broadcasted_iota(jnp.int32, (128, 128), 0)
    col = lax.broadcasted_iota(jnp.int32, (128, 128), 1)

    def orthonormalize():
        inner = exact_dot(image[...], image[...], ((1,), (1,)))
        a[...] = inner
        diagonal[...] = jnp.where(row == col, inner, 0.0)
        inverse_cholesky(a, d)
        lower = jnp.where(col <= row, a[...] * lax.rsqrt(d[...]), 0.0)
        basis[...] = exact_dot(lower, image[...])

    def finish():
        factor_t[...] = basis[...].astype(jnp.bfloat16)
        factor[...] = basis[...].T

    first = exact_dot(start, gram[...])
    first = first * lax.rsqrt(jnp.sum(first * first, axis=1, keepdims=True))
    image[...] = exact_dot(first, gram[...])
    orthonormalize()
    finish()
    kept = jnp.where(row == col, d[...], 1.0) >= 1e-3 * diagonal[...]
    small = jnp.sum(jnp.where(kept, 0.0, 1.0))

    @pl.when(small > 0.0)
    def _():
        basis[...] = start

        def sweep(step, carry):
            image[...] = exact_dot(basis[...], gram[...])
            orthonormalize()
            return carry

        lax.fori_loop(0, ITERS, sweep, 0)
        finish()


VMEM = pl.BlockSpec(memory_space=pltpu.VMEM)
ANY = pl.BlockSpec(memory_space=pl.ANY)
DMA = pltpu.SemaphoreType.DMA


def shards(field, sketch):
    xs, packed = pl.pallas_call(
        gram_kernel,
        out_shape=(
            jax.ShapeDtypeStruct((512, 4096), jnp.bfloat16),
            jax.ShapeDtypeStruct((1280, 128), jnp.float32),
        ),
        in_specs=[pl.BlockSpec(memory_space=pltpu.HBM)],
        out_specs=(VMEM, VMEM),
        scratch_shapes=[
            pltpu.VMEM((GX, 128, 16, 256), jnp.bfloat16),
            pltpu.VMEM((256, 256), jnp.bfloat16),
            pltpu.VMEM((1280, 128), jnp.float32),
            pltpu.VMEM((640, 128), jnp.float32),
            pltpu.VMEM((640, 128), jnp.float32),
            pltpu.VMEM((PLANE, 40, 128), jnp.float32),
            pltpu.VMEM((GZ, 40, 128), jnp.float32),
            DMA((GX * SUB,)), DMA((GX * SUB,)), DMA,
            DMA, DMA,
            DMA((PLANE,)), DMA((PLANE,)),
            DMA((GZ,)), DMA((GZ,)),
            DMA((PLANE,)), DMA((PLANE,)),
            DMA((PLANE,)), DMA((PLANE,)),
        ],
        compiler_params=pltpu.CompilerParams(
            collective_id=0, has_side_effects=True, vmem_limit_bytes=24 * 2**20
        ),
        name="gram",
    )(pltpu.with_memory_space_constraint(field, pltpu.HBM))
    factor, factor_t = pl.pallas_call(
        factor_kernel,
        out_shape=(
            jax.ShapeDtypeStruct((512, 128), jnp.float32),
            jax.ShapeDtypeStruct((128, 512), jnp.bfloat16),
        ),
        in_specs=[VMEM, VMEM],
        out_specs=(VMEM, VMEM),
        scratch_shapes=[
            pltpu.VMEM((512, 512), jnp.float32),
            pltpu.VMEM((128, 512), jnp.float32),
            pltpu.VMEM((128, 512), jnp.float32),
            pltpu.VMEM((128, 128), jnp.float32),
            pltpu.VMEM((128, 128), jnp.float32),
            pltpu.VMEM((128, 128), jnp.float32),
        ],
        compiler_params=pltpu.CompilerParams(vmem_limit_bytes=16 * 2**20),
        name="factor",
    )(packed, sketch)
    core = pl.pallas_call(
        core_kernel,
        out_shape=jax.ShapeDtypeStruct((4, 512, 256), jnp.bfloat16),
        in_specs=[VMEM, VMEM],
        out_specs=VMEM,
        scratch_shapes=[
            pltpu.VMEM((256, 256), jnp.bfloat16),
            pltpu.VMEM((128, 4096), jnp.bfloat16),
            pltpu.VMEM((128, 16, 256), jnp.bfloat16),
            DMA((GX * GY,)), DMA((GX * GY,)), DMA,
        ],
        compiler_params=pltpu.CompilerParams(
            collective_id=1, has_side_effects=True, vmem_limit_bytes=20 * 2**20
        ),
        name="core",
    )(factor_t, xs)
    return (factor, core)


def solution(mesh):
    return jax.shard_map(
        shards,
        mesh=mesh,
        in_specs=(P("gx", "gy", "gz"), P()),
        out_specs=(P(), P(("gx", "gy"), None, "gz")),
        check_vma=False,
    )
```

```python
import functools

import jax
import jax.numpy as jnp
from jax import lax
from jax.experimental import pallas as pl
from jax.experimental.pallas import tpu as pltpu
from jax.sharding import PartitionSpec as P

ITERS = 2
MESH = pl.DeviceIdType.MESH
GX, GY, GZ = 4, 8, 8
YC = GY // 2
PLANE = GX * YC
SUB = 4
FIRST = (0, 128, 384, 768)


def remote(src, dst, send, recv, dev):
    return pltpu.make_async_remote_copy(
        src_ref=src, dst_ref=dst, send_sem=send, recv_sem=recv,
        device_id=dev, device_id_type=MESH,
    )


def swap16():
    row = lax.broadcasted_iota(jnp.int32, (256, 256), 0)
    col = lax.broadcasted_iota(jnp.int32, (256, 256), 1)
    hit = ((row & 15) * 16 + (row >> 4)) == col
    return jnp.where(hit, 1.0, 0.0).astype(jnp.bfloat16)


def gram_kernel(field, xs, gfin, raw, perm, gp, got, acc, r2e, r2l, r3e, r3l, a_send, a_recv, own_sem,
                c_send, c_recv, p_send, p_recv, z_send, z_recv, g_send, g_recv, f_send, f_recv):
    x, y, z = lax.axis_index("gx"), lax.axis_index("gy"), lax.axis_index("gz")
    core, yc = lax.rem(y, 2), lax.div(y, 2)
    other = (x, y + 1 - 2 * core, z)

    def xdev(d):
        return (lax.rem(x + d, GX), y, z)

    def zdev(d):
        return (x, y, lax.rem(z + d, GZ))

    def pdev(d):
        return (lax.rem(x + d // YC, GX), 2 * lax.rem(yc + d % YC, YC) + core, z)

    def pnum(d):
        return lax.rem(x + d // YC + GX, GX) * YC + lax.rem(yc + d % YC, YC)

    def pfrom(d):
        return lax.rem(x - d // YC + GX, GX) * YC + lax.rem(yc - d % YC + YC, YC)

    barrier = pltpu.get_barrier_semaphore()
    peers = [pdev(d) for d in range(1, PLANE)] + [zdev(d) for d in range(1, GZ)] + [other]
    for dev in peers:
        pl.semaphore_signal(barrier, inc=1, device_id=dev, device_id_type=MESH)

    rows, pieces = 32, 16
    mine = pltpu.make_async_copy(
        field.at[:, pl.ds(pl.multiple_of(x * pieces, pieces), pieces), :], raw.at[0], own_sem
    )
    mine.start()
    perm[...] = swap16()
    pl.semaphore_wait(barrier, len(peers))

    sends = {}
    for s in range(SUB):
        for d in (2, 1, 3):
            to = lax.rem(x + d, GX)
            sends[d, s] = remote(
                field.at[pl.ds(s * rows, rows), pl.ds(pl.multiple_of(to * pieces, pieces), pieces), :],
                raw.at[GX - d, pl.ds(s * rows, rows)],
                a_send.at[d * SUB + s], a_recv.at[(GX - d) * SUB + s], xdev(d),
            )
            if s < 2:
                sends[d, s].start()

    def relayout(d, s):
        base = s * 128 + lax.rem(x + d, GX) * rows

        for g in range(rows // 16):
            block = raw[d, s * rows + g * 16:s * rows + g * 16 + 16].reshape(256, 256)
            out = jnp.dot(perm[...], block, preferred_element_type=jnp.float32).astype(jnp.bfloat16)
            for j in range(16):
                xs[pl.ds(pl.multiple_of(base + g * 16, 16), 16), j * 256:(j + 1) * 256] = out[j * 16:(j + 1) * 16]

    def products(s):
        n = 128 * (s + 1)
        at = slice(FIRST[s], FIRST[s] + n)
        for k in range(4):
            cols = slice(k * 1024, (k + 1) * 1024)
            part = lax.dot_general(
                xs[0:n, cols], xs[s * 128:(s + 1) * 128, cols], (((1,), (1,)), ((), ())),
                preferred_element_type=jnp.float32,
            )
            gp[at, :] = part if k == 0 else gp[at, :] + part

    me = pnum(0)
    order = [10, 2, 8, 6, 9, 11, 14, 1, 3, 4, 12, 5, 7, 13, 15]
    pending = []

    def start(copy):
        copy.start()
        pending.append(copy)
        return copy

    class Sum:
        def __init__(self, n, lo, size, r2, r3):
            self.n, self.lo, self.half, self.piece = n, lo, size // 2, size // 2 // PLANE
            self.r2, self.r3 = r2, r3

        def mine(self, which, q=0, size=None):
            first = self.lo + which * self.half + q * self.piece
            return pl.ds(pl.multiple_of(first, 8), self.half if size is None else size)

        def to_core(self):
            self.swap = start(remote(
                gp.at[self.mine(1 - core)], got.at[pl.ds(self.lo // 2, self.half)],
                c_send.at[self.n], c_recv.at[self.n], other,
            ))

        def from_core(self):
            self.swap.wait_recv()
            here = slice(self.lo // 2, self.lo // 2 + self.half)
            acc[here] = gp[self.mine(core)] + got[here]

        def part(self, q):
            return pl.ds(pl.multiple_of(self.lo // 2 + q * self.piece, 8), self.piece)

        def to_plane(self):
            for d in order:
                start(remote(acc.at[self.part(pnum(d))], self.r2.at[me], p_send.at[self.n, d], p_recv.at[self.n, d], pdev(d)))
            self.r2[me] = acc[self.part(me)]

        def from_plane(self):
            for d in order:
                at = self.r2.at[pfrom(d)]
                remote(at, at, p_send.at[self.n, d], p_recv.at[self.n, d], pdev(d)).wait_recv()
            self.r3[z] = total_of([self.r2[q] for q in range(PLANE)])

        def to_line(self):
            for d in (4, 3, 5, 2, 6, 1, 7):
                start(remote(self.r3.at[z], self.r3.at[z], z_send.at[self.n, d], z_recv.at[self.n, d], zdev(d)))

        def from_line(self):
            for d in (1, 7, 2, 6, 3, 5, 4):
                at = self.r3.at[lax.rem(z - d + GZ, GZ)]
                remote(at, at, z_send.at[self.n, d], z_recv.at[self.n, d], zdev(d)).wait_recv()
            gfin[self.mine(core, me, self.piece)] = total_of([self.r3[q] for q in range(GZ)])

        def place(self, which, q):
            return gfin.at[self.mine(which, q, self.piece)]

        def spread(self):
            at = self.place(core, me)
            for d in order:
                start(remote(at, at, g_send.at[self.n, d], g_recv.at[self.n, d], pdev(d)))
            start(remote(at, at, f_send.at[self.n, 0], f_recv.at[self.n, 0], other))

        def gather(self):
            for d in order[::-1]:
                at = self.place(core, pfrom(d))
                remote(at, at, g_send.at[self.n, d], g_recv.at[self.n, d], pdev(d)).wait_recv()
                start(remote(at, at, f_send.at[self.n, d], f_recv.at[self.n, d], other))

        def finish(self):
            for d in range(PLANE):
                at = self.place(1 - core, pfrom(d))
                remote(at, at, f_send.at[self.n, d], f_recv.at[self.n, d], other).wait_recv()

    early, late = Sum(0, 0, 768, r2e, r3e), Sum(1, 768, 512, r2l, r3l)

    mine.wait()
    for s in range(SUB):
        relayout(0, s)
    for s in range(SUB):
        for d in (1, 3, 2):
            sends[GX - d, s].wait_recv()
            if s + 2 < SUB:
                sends[GX - d, s + 2].start()
            relayout(d, s)
        if s == 3:
            early.to_plane()
        products(s)
        if s == 2:
            early.to_core()
            early.from_core()
    late.to_core()
    late.from_core()
    late.to_plane()
    early.from_plane()
    early.to_line()
    late.from_plane()
    late.to_line()
    early.from_line()
    early.spread()
    late.from_line()
    late.spread()
    early.gather()
    late.gather()
    early.finish()
    late.finish()
    for c in list(sends.values()) + pending:
        c.wait_send()


def core_kernel(factor_t, xs, out, perm, t, buf, send, recv, own_sem):
    x, y, z = lax.axis_index("gx"), lax.axis_index("gy"), lax.axis_index("gz")

    def dev(dx, dy):
        return (lax.rem(x + dx, GX), lax.rem(y + dy, GY), z)

    offsets = [(dx, dy) for dx in (2, 1, 3, 0) for dy in (4, 5, 3, 2, 6, 7, 1, 0)]
    barrier = pltpu.get_barrier_semaphore()
    for dx, dy in offsets[:-1]:
        pl.semaphore_signal(barrier, inc=1, device_id=dev(dx, dy), device_id_type=MESH)
    perm[...] = swap16()

    for j in range(16):
        cols = slice(j * 256, (j + 1) * 256)
        t[:, cols] = jnp.dot(factor_t[...], xs[:, cols], preferred_element_type=jnp.float32).astype(jnp.bfloat16)
    for r0 in range(0, 128, 16):
        block = jnp.concatenate([t[r0:r0 + 16, j * 256:(j + 1) * 256] for j in range(16)], axis=0)
        rows = jnp.dot(perm[...], block, preferred_element_type=jnp.float32).astype(jnp.bfloat16)
        buf[r0:r0 + 16] = rows.reshape(16, 16, 256)
    pl.semaphore_wait(barrier, len(offsets) - 1)

    def place(px, py):
        return out.at[:, pl.ds(pl.multiple_of(py * 64 + px * 16, 16), 16), :]

    copies = {}
    for dx, dy in offsets:
        src = buf.at[pl.ds(lax.rem(x + dx, GX) * 32 + lax.rem(y + dy, GY) * 4, 4)]
        if dx or dy:
            n = dx * GY + dy
            copies[n] = remote(src, place(x, y), send.at[n], recv.at[n], dev(dx, dy))
            copies[n].start()
        else:
            mine = pltpu.make_async_copy(src, place(x, y), own_sem)
            mine.start()
    for dx, dy in offsets[:-1]:
        n = dx * GY + dy
        at = place(lax.rem(x - dx + GX, GX), lax.rem(y - dy + GY, GY))
        remote(at, at, send.at[n], recv.at[n], dev(dx, dy)).wait_recv()
    for c in copies.values():
        c.wait_send()
    mine.wait()


def split3(q):
    a = q.astype(jnp.bfloat16).astype(jnp.float32)
    b = (q - a).astype(jnp.bfloat16).astype(jnp.float32)
    return a, b, q - a - b


def total_of(terms):
    while len(terms) > 1:
        terms = [terms[i] + terms[i + 1] if i + 1 < len(terms) else terms[i] for i in range(0, len(terms), 2)]
    return terms[0]


def inverse_cholesky(a, d):
    lane = lax.broadcasted_iota(jnp.int32, (8, 128), 1)
    sub = lax.broadcasted_iota(jnp.int32, (8, 128), 0)

    def repeat(v, l):
        return jnp.broadcast_to(v[:, l:l + 1], (8, 128))

    rows = [jnp.broadcast_to(a[i:i + 1, :], (8, 128)) for i in range(8)]
    for base in range(0, 128, 8):
        inside = (lane >= base) & (lane < base + 8)
        s = [[repeat(rows[i], base + k) for k in range(i + 1)] for i in range(8)]
        w = [jnp.where(inside, jnp.where(lane == base + i, 1.0, 0.0), rows[i]) for i in range(8)]
        inverse = []
        for k in range(8):
            inverse.append(1.0 / s[k][k])
            for i in range(k + 1, 8):
                m = s[i][k] * inverse[k]
                for l in range(k + 1, i + 1):
                    s[i][l] = s[i][l] - m * s[l][k]
                w[i] = w[i] - m * w[k]
        p, scale, pivot = w[0], inverse[0], s[0][0]
        for i in range(1, 8):
            p = jnp.where(sub == i, w[i], p)
            scale = jnp.where(sub == i, inverse[i], scale)
            pivot = jnp.where(sub == i, s[i][i], pivot)
        a[base:base + 8, :] = p
        d[base:base + 8, :] = pivot
        now, after = base + 8, base + 16
        if now < 128:
            before = [jnp.broadcast_to(a[now + i:now + i + 1, :], (8, 128)) for i in range(8)]
            rows = [
                jnp.where(inside, 0.0, before[i])
                - total_of([repeat(w[k], now + i) * inverse[k] * w[k] for k in range(8)])
                for i in range(8)
            ]
        if after < 128:
            u, v = split3(p), split3(p * scale)
            left = jnp.concatenate([u[0], u[0], u[1], u[0], u[1], u[2]], axis=0).astype(jnp.bfloat16)
            right = jnp.concatenate([v[0], v[1], v[0], v[2], v[1], v[0]], axis=0).astype(jnp.bfloat16)
            change = lax.dot_general(left, right, (((0,), (0,)), ((), ())), preferred_element_type=jnp.float32)
            old = a[after:, :]
            a[after:, :] = jnp.where(jnp.broadcast_to(inside[:1], old.shape), 0.0, old) - change[after:, :]


def exact_dot(u, v, dims=((1,), (0,))):
    return lax.dot_general(u, v, (dims, ((), ())), precision=lax.Precision.HIGHEST, preferred_element_type=jnp.float32)


def factor_kernel(packed, sketch, factor, factor_t, gram, basis, image, a, d, diagonal):
    for s in range(SUB):
        for r in range(s + 1):
            block = packed[FIRST[s] + 128 * r:FIRST[s] + 128 * r + 128, :]
            gram[128 * r:128 * r + 128, 128 * s:128 * s + 128] = block
            if r < s:
                gram[128 * s:128 * s + 128, 128 * r:128 * r + 128] = block.T
    start = jnp.concatenate(
        [sketch[128 * b + 32 * s:128 * b + 32 * s + 32, :] for s in range(SUB) for b in range(GX)], axis=0
    ).T
    row = lax.broadcasted_iota(jnp.int32, (128, 128), 0)
    col = lax.broadcasted_iota(jnp.int32, (128, 128), 1)

    def orthonormalize():
        inner = exact_dot(image[...], image[...], ((1,), (1,)))
        a[...] = inner
        diagonal[...] = jnp.where(row == col, inner, 0.0)
        inverse_cholesky(a, d)
        lower = jnp.where(col <= row, a[...] * lax.rsqrt(d[...]), 0.0)
        basis[...] = exact_dot(lower, image[...])

    def finish():
        factor_t[...] = basis[...].astype(jnp.bfloat16)
        final = basis[...].T
        for s in range(SUB):
            for b in range(GX):
                factor[128 * b + 32 * s:128 * b + 32 * s + 32, :] = final[128 * s + 32 * b:128 * s + 32 * b + 32, :]

    first = exact_dot(start, gram[...])
    first = first * lax.rsqrt(jnp.sum(first * first, axis=1, keepdims=True))
    image[...] = exact_dot(first, gram[...])
    orthonormalize()
    finish()
    kept = jnp.where(row == col, d[...], 1.0) >= 1e-3 * diagonal[...]
    small = jnp.sum(jnp.where(kept, 0.0, 1.0))

    @pl.when(small > 0.0)
    def _():
        basis[...] = start

        def sweep(step, carry):
            image[...] = exact_dot(basis[...], gram[...])
            orthonormalize()
            return carry

        lax.fori_loop(0, ITERS, sweep, 0)
        finish()


VMEM = pl.BlockSpec(memory_space=pltpu.VMEM)
ANY = pl.BlockSpec(memory_space=pl.ANY)
DMA = pltpu.SemaphoreType.DMA


def shards(field, sketch):
    xs, packed = pl.pallas_call(
        gram_kernel,
        out_shape=(
            jax.ShapeDtypeStruct((512, 4096), jnp.bfloat16),
            jax.ShapeDtypeStruct((1280, 128), jnp.float32),
        ),
        in_specs=[pl.BlockSpec(memory_space=pltpu.HBM)],
        out_specs=(VMEM, VMEM),
        scratch_shapes=[
            pltpu.VMEM((GX, 128, 16, 256), jnp.bfloat16),
            pltpu.VMEM((256, 256), jnp.bfloat16),
            pltpu.VMEM((1280, 128), jnp.float32),
            pltpu.VMEM((640, 128), jnp.float32),
            pltpu.VMEM((640, 128), jnp.float32),
            pltpu.VMEM((PLANE, 24, 128), jnp.float32),
            pltpu.VMEM((PLANE, 16, 128), jnp.float32),
            pltpu.VMEM((GZ, 24, 128), jnp.float32),
            pltpu.VMEM((GZ, 16, 128), jnp.float32),
            DMA((GX * SUB,)), DMA((GX * SUB,)), DMA,
            DMA((2,)), DMA((2,)),
            DMA((2, PLANE)), DMA((2, PLANE)),
            DMA((2, GZ)), DMA((2, GZ)),
            DMA((2, PLANE)), DMA((2, PLANE)),
            DMA((2, PLANE)), DMA((2, PLANE)),
        ],
        compiler_params=pltpu.CompilerParams(
            collective_id=0, has_side_effects=True, vmem_limit_bytes=24 * 2**20
        ),
        name="gram",
    )(pltpu.with_memory_space_constraint(field, pltpu.HBM))
    factor, factor_t = pl.pallas_call(
        factor_kernel,
        out_shape=(
            jax.ShapeDtypeStruct((512, 128), jnp.float32),
            jax.ShapeDtypeStruct((128, 512), jnp.bfloat16),
        ),
        in_specs=[VMEM, VMEM],
        out_specs=(VMEM, VMEM),
        scratch_shapes=[
            pltpu.VMEM((512, 512), jnp.float32),
            pltpu.VMEM((128, 512), jnp.float32),
            pltpu.VMEM((128, 512), jnp.float32),
            pltpu.VMEM((128, 128), jnp.float32),
            pltpu.VMEM((128, 128), jnp.float32),
            pltpu.VMEM((128, 128), jnp.float32),
        ],
        compiler_params=pltpu.CompilerParams(vmem_limit_bytes=16 * 2**20),
        name="factor",
    )(packed, sketch)
    core = pl.pallas_call(
        core_kernel,
        out_shape=jax.ShapeDtypeStruct((4, 512, 256), jnp.bfloat16),
        in_specs=[VMEM, VMEM],
        out_specs=VMEM,
        scratch_shapes=[
            pltpu.VMEM((256, 256), jnp.bfloat16),
            pltpu.VMEM((128, 4096), jnp.bfloat16),
            pltpu.VMEM((128, 16, 256), jnp.bfloat16),
            DMA((GX * GY,)), DMA((GX * GY,)), DMA,
        ],
        compiler_params=pltpu.CompilerParams(
            collective_id=1, has_side_effects=True, vmem_limit_bytes=20 * 2**20
        ),
        name="core",
    )(factor_t, xs)
    return (factor, core)


def solution(mesh):
    return jax.shard_map(
        shards,
        mesh=mesh,
        in_specs=(P("gx", "gy", "gz"), P()),
        out_specs=(P(), P(("gx", "gy"), None, "gz")),
        check_vma=False,
    )
```

```python
import functools

import jax
import jax.numpy as jnp
from jax import lax
from jax.experimental import pallas as pl
from jax.experimental.pallas import tpu as pltpu
from jax.sharding import PartitionSpec as P

ITERS = 2
MESH = pl.DeviceIdType.MESH
GX, GY, GZ = 4, 8, 8
YC = GY // 2
PLANE = GX * YC
SUB = 4
FIRST = (0, 128, 384, 768)


def remote(src, dst, send, recv, dev):
    return pltpu.make_async_remote_copy(
        src_ref=src, dst_ref=dst, send_sem=send, recv_sem=recv,
        device_id=dev, device_id_type=MESH,
    )


def swap16():
    row = lax.broadcasted_iota(jnp.int32, (256, 256), 0)
    col = lax.broadcasted_iota(jnp.int32, (256, 256), 1)
    hit = ((row & 15) * 16 + (row >> 4)) == col
    return jnp.where(hit, 1.0, 0.0).astype(jnp.bfloat16)


def gram_kernel(field, xs, gfin, raw, perm, gp, got, acc, r2e, r2l, r3e, r3l, a_send, a_recv, own_sem,
                c_send, c_recv, p_send, p_recv, z_send, z_recv, g_send, g_recv, f_send, f_recv):
    x, y, z = lax.axis_index("gx"), lax.axis_index("gy"), lax.axis_index("gz")
    core, yc = lax.rem(y, 2), lax.div(y, 2)
    other = (x, y + 1 - 2 * core, z)

    def xdev(d):
        return (lax.rem(x + d, GX), y, z)

    def zdev(d):
        return (x, y, lax.rem(z + d, GZ))

    def pdev(d):
        return (lax.rem(x + d // YC, GX), 2 * lax.rem(yc + d % YC, YC) + core, z)

    def pnum(d):
        return lax.rem(x + d // YC + GX, GX) * YC + lax.rem(yc + d % YC, YC)

    def pfrom(d):
        return lax.rem(x - d // YC + GX, GX) * YC + lax.rem(yc - d % YC + YC, YC)

    barrier = pltpu.get_barrier_semaphore()
    peers = [pdev(d) for d in (8, 4, 12, 10, 2, 6, 9, 11, 14, 1, 3, 5, 7, 13, 15)] + [zdev(d) for d in (4, 3, 5, 2, 6, 1, 7)]
    for dev in peers + [other]:
        pl.semaphore_signal(barrier, inc=1, device_id=dev, device_id_type=MESH)

    rows, pieces = 32, 16
    pl.semaphore_wait(barrier, len(peers) + 1)

    sends = {}
    for s in range(SUB):
        for d in (2, 1, 3):
            to = lax.rem(x + d, GX)
            sends[d, s] = remote(
                field.at[pl.ds(s * rows, rows), pl.ds(pl.multiple_of(to * pieces, pieces), pieces), :],
                raw.at[GX - d, pl.ds(s * rows, rows)],
                a_send.at[d * SUB + s], a_recv.at[(GX - d) * SUB + s], xdev(d),
            )
            if s < 2:
                sends[d, s].start()
    mine = pltpu.make_async_copy(
        field.at[:, pl.ds(pl.multiple_of(x * pieces, pieces), pieces), :], raw.at[0], own_sem
    )
    mine.start()
    perm[...] = swap16()

    def relayout(d, s):
        base = s * 128 + lax.rem(x + d, GX) * rows

        for g in range(rows // 16):
            block = raw[d, s * rows + g * 16:s * rows + g * 16 + 16].reshape(256, 256)
            out = jnp.dot(perm[...], block, preferred_element_type=jnp.float32).astype(jnp.bfloat16)
            for j in range(16):
                xs[pl.ds(pl.multiple_of(base + g * 16, 16), 16), j * 256:(j + 1) * 256] = out[j * 16:(j + 1) * 16]

    def products(s):
        n = 128 * (s + 1)
        at = slice(FIRST[s], FIRST[s] + n)
        for k in range(4):
            cols = slice(k * 1024, (k + 1) * 1024)
            part = lax.dot_general(
                xs[0:n, cols], xs[s * 128:(s + 1) * 128, cols], (((1,), (1,)), ((), ())),
                preferred_element_type=jnp.float32,
            )
            gp[at, :] = part if k == 0 else gp[at, :] + part

    me = pnum(0)
    order = [10, 2, 8, 6, 9, 11, 14, 1, 3, 4, 12, 5, 7, 13, 15]
    pending = []

    def start(copy):
        copy.start()
        pending.append(copy)
        return copy

    def settle():
        while pending:
            pending.pop(0).wait_send()

    class Sum:
        def __init__(self, n, lo, size, r2, r3):
            self.n, self.lo, self.half, self.piece = n, lo, size // 2, size // 2 // PLANE
            self.r2, self.r3 = r2, r3

        def mine(self, which, q=0, size=None):
            first = self.lo + which * self.half + q * self.piece
            return pl.ds(pl.multiple_of(first, 8), self.half if size is None else size)

        def to_core(self):
            self.swap = start(remote(
                gp.at[self.mine(1 - core)], got.at[pl.ds(self.lo // 2, self.half)],
                c_send.at[self.n], c_recv.at[self.n], other,
            ))

        def from_core(self):
            self.swap.wait_recv()
            here = slice(self.lo // 2, self.lo // 2 + self.half)
            acc[here] = gp[self.mine(core)] + got[here]

        def part(self, q):
            return pl.ds(pl.multiple_of(self.lo // 2 + q * self.piece, 8), self.piece)

        def to_plane(self):
            for d in order:
                start(remote(acc.at[self.part(pnum(d))], self.r2.at[me], p_send.at[self.n, d], p_recv.at[self.n, d], pdev(d)))
            self.r2[me] = acc[self.part(me)]

        def from_plane(self):
            for d in order:
                at = self.r2.at[pfrom(d)]
                remote(at, at, p_send.at[self.n, d], p_recv.at[self.n, d], pdev(d)).wait_recv()
            self.r3[z] = total_of([self.r2[q] for q in range(PLANE)])

        def to_line(self):
            for d in (4, 3, 5, 2, 6, 1, 7):
                start(remote(self.r3.at[z], self.r3.at[z], z_send.at[self.n, d], z_recv.at[self.n, d], zdev(d)))

        def from_line(self):
            for d in (1, 7, 2, 6, 3, 5, 4):
                at = self.r3.at[lax.rem(z - d + GZ, GZ)]
                remote(at, at, z_send.at[self.n, d], z_recv.at[self.n, d], zdev(d)).wait_recv()
            gfin[self.mine(core, me, self.piece)] = total_of([self.r3[q] for q in range(GZ)])

        def place(self, which, q):
            return gfin.at[self.mine(which, q, self.piece)]

        def spread(self):
            at = self.place(core, me)
            for d in order:
                start(remote(at, at, g_send.at[self.n, d], g_recv.at[self.n, d], pdev(d)))

        def row(self, which, dx):
            first = self.lo + which * self.half + lax.rem(x - dx + GX, GX) * YC * self.piece
            return gfin.at[pl.ds(pl.multiple_of(first, 8), YC * self.piece)]

        def gather(self):
            for dx in (0, 1, 3, 2):
                for dy in range(YC):
                    d = dx * YC + dy
                    if d:
                        at = self.place(core, pfrom(d))
                        remote(at, at, g_send.at[self.n, d], g_recv.at[self.n, d], pdev(d)).wait_recv()
                at = self.row(core, dx)
                start(remote(at, at, f_send.at[self.n, dx], f_recv.at[self.n, dx], other))

        def finish(self):
            for dx in (0, 1, 3, 2):
                at = self.row(1 - core, dx)
                remote(at, at, f_send.at[self.n, dx], f_recv.at[self.n, dx], other).wait_recv()

    early, late = Sum(0, 0, 768, r2e, r3e), Sum(1, 768, 512, r2l, r3l)

    mine.wait()
    for s in range(SUB):
        relayout(0, s)
    for s in range(SUB):
        for d in (1, 3, 2):
            sends[GX - d, s].wait_recv()
            if s + 2 < SUB:
                sends[GX - d, s + 2].start()
            relayout(d, s)
            if s == 3 and d == 1:
                early.to_plane()
        products(s)
        if s == 2:
            early.to_core()
            early.from_core()
    late.to_core()
    late.from_core()
    late.to_plane()
    early.from_plane()
    early.to_line()
    late.from_plane()
    late.to_line()
    early.from_line()
    early.spread()
    for c in sends.values():
        c.wait_send()
    settle()
    late.from_line()
    late.spread()
    early.gather()
    early.finish()
    settle()
    late.gather()
    settle()
    late.finish()


def core_kernel(factor_t, xs, out, perm, t, buf, send, recv, own_sem, ready):
    x, y, z = lax.axis_index("gx"), lax.axis_index("gy"), lax.axis_index("gz")
    core, yc = lax.rem(y, 2), lax.div(y, 2)

    def there(dx, dy, f):
        flip = 1 - core if f else core
        return lax.rem(x + dx + GX, GX), 2 * lax.rem(yc + dy + YC, YC) + flip

    def dev(dx, dy, f):
        return (*there(dx, dy, f), z)

    def hops(dx, dy):
        return min(dx, GX - dx) + min(dy, YC - dy)

    offsets = [(dx, dy, f) for dx in range(GX) for dy in range(YC) for f in range(2) if dx or dy or f]
    near = sorted((o for o in offsets if hops(*o[:2]) <= 2), key=lambda o: -hops(*o[:2]))
    far = sorted((o for o in offsets if hops(*o[:2]) > 2), key=lambda o: -hops(*o[:2]))
    corners = [dev(1, 1, 0), dev(3, 3, 0)]
    barrier = pltpu.get_barrier_semaphore()
    for o in near:
        pl.semaphore_signal(barrier, inc=1, device_id=dev(*o), device_id_type=MESH)
    perm[...] = swap16()

    for j in range(16):
        cols = slice(j * 256, (j + 1) * 256)
        t[:, cols] = jnp.dot(factor_t[...], xs[:, cols], preferred_element_type=jnp.float32).astype(jnp.bfloat16)
    for r0 in range(0, 128, 16):
        block = jnp.concatenate([t[r0:r0 + 16, j * 256:(j + 1) * 256] for j in range(16)], axis=0)
        rows = jnp.dot(perm[...], block, preferred_element_type=jnp.float32).astype(jnp.bfloat16)
        buf[r0:r0 + 16] = rows.reshape(16, 16, 256)
    pl.semaphore_wait(barrier, len(near))
    for corner in corners:
        pl.semaphore_signal(ready, inc=1, device_id=corner, device_id_type=MESH)

    def place(px, py):
        return out.at[:, pl.ds(pl.multiple_of(py * 64 + px * 16, 16), 16), :]

    def number(dx, dy, f):
        return (dx * YC + dy) * 2 + f

    copies = []

    def push(o):
        px, py = there(*o)
        src = buf.at[pl.ds(px * 32 + py * 4, 4)]
        copies.append(remote(src, place(x, y), send.at[number(*o)], recv.at[number(*o)], dev(*o)))
        copies[-1].start()

    two = [o for o in near if hops(*o[:2]) == 2]
    for o in two:
        push(o)
    pl.semaphore_wait(ready, len(corners))
    for o in far + near[len(two):]:
        push(o)
    mine = pltpu.make_async_copy(buf.at[pl.ds(x * 32 + y * 4, 4)], place(x, y), own_sem)
    mine.start()
    for c in copies:
        c.wait_send()
    for dx, dy, f in near + far:
        at = place(*there(-dx, -dy, f))
        n = number(dx, dy, f)
        remote(at, at, send.at[n], recv.at[n], dev(dx, dy, f)).wait_recv()
    mine.wait()


def split3(q):
    a = q.astype(jnp.bfloat16).astype(jnp.float32)
    b = (q - a).astype(jnp.bfloat16).astype(jnp.float32)
    return a, b, q - a - b


def total_of(terms):
    while len(terms) > 1:
        terms = [terms[i] + terms[i + 1] if i + 1 < len(terms) else terms[i] for i in range(0, len(terms), 2)]
    return terms[0]


def inverse_cholesky(a, d):
    lane = lax.broadcasted_iota(jnp.int32, (8, 128), 1)
    sub = lax.broadcasted_iota(jnp.int32, (8, 128), 0)

    def repeat(v, l):
        return jnp.broadcast_to(v[:, l:l + 1], (8, 128))

    rows = [jnp.broadcast_to(a[i:i + 1, :], (8, 128)) for i in range(8)]
    for base in range(0, 128, 8):
        inside = (lane >= base) & (lane < base + 8)
        s = [[repeat(rows[i], base + k) for k in range(i + 1)] for i in range(8)]
        w = [jnp.where(inside, jnp.where(lane == base + i, 1.0, 0.0), rows[i]) for i in range(8)]
        inverse = []
        for k in range(8):
            inverse.append(1.0 / s[k][k])
            for i in range(k + 1, 8):
                m = s[i][k] * inverse[k]
                for l in range(k + 1, i + 1):
                    s[i][l] = s[i][l] - m * s[l][k]
                w[i] = w[i] - m * w[k]
        p, scale, pivot = w[0], inverse[0], s[0][0]
        for i in range(1, 8):
            p = jnp.where(sub == i, w[i], p)
            scale = jnp.where(sub == i, inverse[i], scale)
            pivot = jnp.where(sub == i, s[i][i], pivot)
        a[base:base + 8, :] = p
        d[base:base + 8, :] = pivot
        now, after = base + 8, base + 16
        if now < 128:
            before = [jnp.broadcast_to(a[now + i:now + i + 1, :], (8, 128)) for i in range(8)]
            rows = [
                jnp.where(inside, 0.0, before[i])
                - total_of([repeat(w[k], now + i) * inverse[k] * w[k] for k in range(8)])
                for i in range(8)
            ]
        if after < 128:
            u, v = split3(p), split3(p * scale)
            left = jnp.concatenate([u[0], u[0], u[1], u[0], u[1], u[2]], axis=0).astype(jnp.bfloat16)
            right = jnp.concatenate([v[0], v[1], v[0], v[2], v[1], v[0]], axis=0).astype(jnp.bfloat16)
            change = lax.dot_general(left, right, (((0,), (0,)), ((), ())), preferred_element_type=jnp.float32)
            old = a[after:, :]
            a[after:, :] = jnp.where(jnp.broadcast_to(inside[:1], old.shape), 0.0, old) - change[after:, :]


def exact_dot(u, v, dims=((1,), (0,))):
    return lax.dot_general(u, v, (dims, ((), ())), precision=lax.Precision.HIGHEST, preferred_element_type=jnp.float32)


def factor_kernel(packed, sketch, factor, factor_t, gram, basis, image, a, d, diagonal):
    for s in range(SUB):
        for r in range(s + 1):
            block = packed[FIRST[s] + 128 * r:FIRST[s] + 128 * r + 128, :]
            gram[128 * r:128 * r + 128, 128 * s:128 * s + 128] = block
            if r < s:
                gram[128 * s:128 * s + 128, 128 * r:128 * r + 128] = block.T
    start = jnp.concatenate(
        [sketch[128 * b + 32 * s:128 * b + 32 * s + 32, :] for s in range(SUB) for b in range(GX)], axis=0
    ).T
    row = lax.broadcasted_iota(jnp.int32, (128, 128), 0)
    col = lax.broadcasted_iota(jnp.int32, (128, 128), 1)

    def orthonormalize():
        inner = exact_dot(image[...], image[...], ((1,), (1,)))
        a[...] = inner
        diagonal[...] = jnp.where(row == col, inner, 0.0)
        inverse_cholesky(a, d)
        lower = jnp.where(col <= row, a[...] * lax.rsqrt(d[...]), 0.0)
        basis[...] = exact_dot(lower, image[...])

    def finish():
        factor_t[...] = basis[...].astype(jnp.bfloat16)
        final = basis[...].T
        for s in range(SUB):
            for b in range(GX):
                factor[128 * b + 32 * s:128 * b + 32 * s + 32, :] = final[128 * s + 32 * b:128 * s + 32 * b + 32, :]

    first = exact_dot(start, gram[...])
    first = first * lax.rsqrt(jnp.sum(first * first, axis=1, keepdims=True))
    image[...] = exact_dot(first, gram[...])
    orthonormalize()
    finish()
    kept = jnp.where(row == col, d[...], 1.0) >= 1e-3 * diagonal[...]
    small = jnp.sum(jnp.where(kept, 0.0, 1.0))

    @pl.when(small > 0.0)
    def _():
        basis[...] = start

        def sweep(step, carry):
            image[...] = exact_dot(basis[...], gram[...])
            orthonormalize()
            return carry

        lax.fori_loop(0, ITERS, sweep, 0)
        finish()


VMEM = pl.BlockSpec(memory_space=pltpu.VMEM)
ANY = pl.BlockSpec(memory_space=pl.ANY)
DMA = pltpu.SemaphoreType.DMA


def shards(field, sketch):
    xs, packed = pl.pallas_call(
        gram_kernel,
        out_shape=(
            jax.ShapeDtypeStruct((512, 4096), jnp.bfloat16),
            jax.ShapeDtypeStruct((1280, 128), jnp.float32),
        ),
        in_specs=[pl.BlockSpec(memory_space=pltpu.HBM)],
        out_specs=(VMEM, VMEM),
        scratch_shapes=[
            pltpu.VMEM((GX, 128, 16, 256), jnp.bfloat16),
            pltpu.VMEM((256, 256), jnp.bfloat16),
            pltpu.VMEM((1280, 128), jnp.float32),
            pltpu.VMEM((640, 128), jnp.float32),
            pltpu.VMEM((640, 128), jnp.float32),
            pltpu.VMEM((PLANE, 24, 128), jnp.float32),
            pltpu.VMEM((PLANE, 16, 128), jnp.float32),
            pltpu.VMEM((GZ, 24, 128), jnp.float32),
            pltpu.VMEM((GZ, 16, 128), jnp.float32),
            DMA((GX * SUB,)), DMA((GX * SUB,)), DMA,
            DMA((2,)), DMA((2,)),
            DMA((2, PLANE)), DMA((2, PLANE)),
            DMA((2, GZ)), DMA((2, GZ)),
            DMA((2, PLANE)), DMA((2, PLANE)),
            DMA((2, GX)), DMA((2, GX)),
        ],
        compiler_params=pltpu.CompilerParams(
            collective_id=0, has_side_effects=True, vmem_limit_bytes=24 * 2**20
        ),
        name="gram",
    )(pltpu.with_memory_space_constraint(field, pltpu.HBM))
    factor, factor_t = pl.pallas_call(
        factor_kernel,
        out_shape=(
            jax.ShapeDtypeStruct((512, 128), jnp.float32),
            jax.ShapeDtypeStruct((128, 512), jnp.bfloat16),
        ),
        in_specs=[VMEM, VMEM],
        out_specs=(VMEM, VMEM),
        scratch_shapes=[
            pltpu.VMEM((512, 512), jnp.float32),
            pltpu.VMEM((128, 512), jnp.float32),
            pltpu.VMEM((128, 512), jnp.float32),
            pltpu.VMEM((128, 128), jnp.float32),
            pltpu.VMEM((128, 128), jnp.float32),
            pltpu.VMEM((128, 128), jnp.float32),
        ],
        compiler_params=pltpu.CompilerParams(vmem_limit_bytes=16 * 2**20),
        name="factor",
    )(packed, sketch)
    core = pl.pallas_call(
        core_kernel,
        out_shape=jax.ShapeDtypeStruct((4, 512, 256), jnp.bfloat16),
        in_specs=[VMEM, VMEM],
        out_specs=VMEM,
        scratch_shapes=[
            pltpu.VMEM((256, 256), jnp.bfloat16),
            pltpu.VMEM((128, 4096), jnp.bfloat16),
            pltpu.VMEM((128, 16, 256), jnp.bfloat16),
            DMA((GX * GY,)), DMA((GX * GY,)), DMA,
            pltpu.SemaphoreType.REGULAR,
        ],
        compiler_params=pltpu.CompilerParams(
            collective_id=1, has_side_effects=True, vmem_limit_bytes=20 * 2**20
        ),
        name="core",
    )(factor_t, xs)
    return (factor, core)


def solution(mesh):
    return jax.shard_map(
        shards,
        mesh=mesh,
        in_specs=(P("gx", "gy", "gz"), P()),
        out_specs=(P(), P(("gx", "gy"), None, "gz")),
        check_vma=False,
    )
```

```python
import functools

import jax
import jax.numpy as jnp
from jax import lax
from jax.experimental import pallas as pl
from jax.experimental.pallas import tpu as pltpu
from jax.sharding import PartitionSpec as P

ITERS = 2
MESH = pl.DeviceIdType.MESH
GX, GY, GZ = 4, 8, 8
YC = GY // 2
PLANE = GX * YC
LENGTH = (32, 32, 32, 16, 16)
START = (0, 32, 64, 96, 112)
BASE = (0, 128, 256, 384, 448)
LAST = 4
FIRST = (0, 128, 384, 768, 1024)
PARTS = ((0, (0, 1)), (1, (0, 1)), (2, (0, 1)), (3, (0, 1)), (4, (0,)), (4, (1,)))
AHEAD = 6


def remote(src, dst, send, recv, dev):
    return pltpu.make_async_remote_copy(
        src_ref=src, dst_ref=dst, send_sem=send, recv_sem=recv,
        device_id=dev, device_id_type=MESH,
    )


def swap16():
    row = lax.broadcasted_iota(jnp.int32, (256, 256), 0)
    col = lax.broadcasted_iota(jnp.int32, (256, 256), 1)
    hit = ((row & 15) * 16 + (row >> 4)) == col
    return jnp.where(hit, 1.0, 0.0).astype(jnp.bfloat16)


def gram_kernel(field, xs, gfin, raw, perm, gp, got, acc, r2e, r2l, r3e, r3l, a_send, a_recv, own_sem,
                c_send, c_recv, p_send, p_recv, z_send, z_recv, g_send, g_recv, f_send, f_recv):
    x, y, z = lax.axis_index("gx"), lax.axis_index("gy"), lax.axis_index("gz")
    core, yc = lax.rem(y, 2), lax.div(y, 2)
    other = (x, y + 1 - 2 * core, z)

    def xdev(d):
        return (lax.rem(x + d, GX), y, z)

    def zdev(d):
        return (x, y, lax.rem(z + d, GZ))

    def pdev(d):
        return (lax.rem(x + d // YC, GX), 2 * lax.rem(yc + d % YC, YC) + core, z)

    def pnum(d):
        return lax.rem(x + d // YC + GX, GX) * YC + lax.rem(yc + d % YC, YC)

    def pfrom(d):
        return lax.rem(x - d // YC + GX, GX) * YC + lax.rem(yc - d % YC + YC, YC)

    barrier = pltpu.get_barrier_semaphore()
    peers = [pdev(d) for d in (8, 4, 12, 10, 2, 6, 9, 11, 14, 1, 3, 5, 7, 13, 15)] + [zdev(d) for d in (4, 3, 5, 2, 6, 1, 7)]
    for dev in peers + [other]:
        pl.semaphore_signal(barrier, inc=1, device_id=dev, device_id_type=MESH)

    pieces = 16
    pl.semaphore_wait(barrier, len(peers) + 1)

    sends = {}
    for m, (k, halves) in enumerate(PARTS):
        rows = pl.ds(START[k], LENGTH[k])
        cols = pl.ds(halves[0] * 128, len(halves) * 128)
        for d in (2, 1, 3):
            to = lax.rem(x + d, GX)
            sends[d, m] = remote(
                field.at[rows, pl.ds(pl.multiple_of(to * pieces, pieces), pieces), cols],
                raw.at[GX - d, rows, :, cols],
                a_send.at[d * len(PARTS) + m], a_recv.at[(GX - d) * len(PARTS) + m], xdev(d),
            )
            if m < AHEAD:
                sends[d, m].start()
    mine = pltpu.make_async_copy(
        field.at[:, pl.ds(pl.multiple_of(x * pieces, pieces), pieces), :], raw.at[0], own_sem
    )
    mine.start()
    perm[...] = swap16()

    def relayout(d, m):
        k, halves = PARTS[m]
        base = BASE[k] + lax.rem(x + d, GX) * LENGTH[k]
        for g in range(0, LENGTH[k], 16):
            block = raw[d, START[k] + g:START[k] + g + 16, :, halves[0] * 128:halves[-1] * 128 + 128]
            block = block.reshape(256, 128 * len(halves))
            out = jnp.dot(perm[...], block, preferred_element_type=jnp.float32).astype(jnp.bfloat16)
            for n, h in enumerate(halves):
                for j in range(16):
                    xs[pl.ds(pl.multiple_of(base + g, 16), 16), h * 2048 + j * 128:h * 2048 + j * 128 + 128] = (
                        out[j * 16:(j + 1) * 16, n * 128:(n + 1) * 128]
                    )

    left_lanes = lax.broadcasted_iota(jnp.int32, (1, 128), 1) < 64

    def products(m):
        k, halves = PARTS[m]
        wide = 4 * LENGTH[k]
        n = BASE[k] + wide
        for step in range(2 * halves[0], 2 * halves[-1] + 2):
            cols = slice(step * 1024, (step + 1) * 1024)
            right = xs[BASE[k]:n, cols]
            if wide == 64:
                right = jnp.concatenate([right, right], axis=0)
            part = lax.dot_general(
                xs[0:n, cols], right, (((1,), (1,)), ((), ())), preferred_element_type=jnp.float32
            )
            if wide == 64:
                part = jnp.where(left_lanes, part[:n // 2], part[n // 2:])
            at = slice(FIRST[k], FIRST[k] + part.shape[0])
            gp[at, :] = part if step == 0 else gp[at, :] + part

    me = pnum(0)
    order = [10, 2, 8, 6, 9, 11, 14, 1, 3, 4, 12, 5, 7, 13, 15]
    pending = []

    def start(copy):
        copy.start()
        pending.append(copy)
        return copy

    def settle():
        while pending:
            pending.pop(0).wait_send()

    class Sum:
        def __init__(self, n, lo, size, r2, r3):
            self.n, self.lo, self.half, self.piece = n, lo, size // 2, size // 2 // PLANE
            self.r2, self.r3 = r2, r3

        def mine(self, which, q=0, size=None):
            first = self.lo + which * self.half + q * self.piece
            return pl.ds(pl.multiple_of(first, 8), self.half if size is None else size)

        def to_core(self):
            self.swap = start(remote(
                gp.at[self.mine(1 - core)], got.at[pl.ds(self.lo // 2, self.half)],
                c_send.at[self.n], c_recv.at[self.n], other,
            ))

        def from_core(self):
            self.swap.wait_recv()
            here = slice(self.lo // 2, self.lo // 2 + self.half)
            acc[here] = gp[self.mine(core)] + got[here]

        def part(self, q):
            return pl.ds(pl.multiple_of(self.lo // 2 + q * self.piece, 8), self.piece)

        def to_plane(self):
            for d in order:
                start(remote(acc.at[self.part(pnum(d))], self.r2.at[me], p_send.at[self.n, d], p_recv.at[self.n, d], pdev(d)))
            self.r2[me] = acc[self.part(me)]

        def from_plane(self):
            for d in order:
                at = self.r2.at[pfrom(d)]
                remote(at, at, p_send.at[self.n, d], p_recv.at[self.n, d], pdev(d)).wait_recv()
            self.r3[z] = total_of([self.r2[q] for q in range(PLANE)])

        def to_line(self):
            for d in (4, 3, 5, 2, 6, 1, 7):
                start(remote(self.r3.at[z], self.r3.at[z], z_send.at[self.n, d], z_recv.at[self.n, d], zdev(d)))

        def from_line(self):
            for d in (1, 7, 2, 6, 3, 5, 4):
                at = self.r3.at[lax.rem(z - d + GZ, GZ)]
                remote(at, at, z_send.at[self.n, d], z_recv.at[self.n, d], zdev(d)).wait_recv()
            gfin[self.mine(core, me, self.piece)] = total_of([self.r3[q] for q in range(GZ)])

        def place(self, which, q):
            return gfin.at[self.mine(which, q, self.piece)]

        def spread(self):
            at = self.place(core, me)
            for d in order:
                start(remote(at, at, g_send.at[self.n, d], g_recv.at[self.n, d], pdev(d)))

        def row(self, which, dx):
            first = self.lo + which * self.half + lax.rem(x - dx + GX, GX) * YC * self.piece
            return gfin.at[pl.ds(pl.multiple_of(first, 8), YC * self.piece)]

        def gather(self):
            for dx in (0, 1, 3, 2):
                for dy in range(YC):
                    d = dx * YC + dy
                    if d:
                        at = self.place(core, pfrom(d))
                        remote(at, at, g_send.at[self.n, d], g_recv.at[self.n, d], pdev(d)).wait_recv()
                at = self.row(core, dx)
                start(remote(at, at, f_send.at[self.n, dx], f_recv.at[self.n, dx], other))

        def finish(self):
            for dx in (0, 1, 3, 2):
                at = self.row(1 - core, dx)
                remote(at, at, f_send.at[self.n, dx], f_recv.at[self.n, dx], other).wait_recv()

    early, late = Sum(0, 0, 768, r2e, r3e), Sum(1, 768, 512, r2l, r3l)
    gp[992:1024, :] = jnp.zeros((32, 128), jnp.float32)

    mine.wait()
    for m in range(len(PARTS)):
        relayout(0, m)
    for m in range(len(PARTS)):
        for d in (1, 3, 2):
            sends[GX - d, m].wait_recv()
            if m + AHEAD < len(PARTS):
                sends[GX - d, m + AHEAD].start()
            relayout(d, m)
        products(m)
        if m == 2:
            early.to_core()
            early.from_core()
            early.to_plane()
    late.to_core()
    late.from_core()
    late.to_plane()
    early.from_plane()
    early.to_line()
    late.from_plane()
    late.to_line()
    early.from_line()
    early.spread()
    for c in sends.values():
        c.wait_send()
    settle()
    late.from_line()
    late.spread()
    early.gather()
    early.finish()
    settle()
    late.gather()
    settle()
    late.finish()


def core_kernel(factor_t, xs, out, perm, t, buf, send, recv, own_sem, ready):
    x, y, z = lax.axis_index("gx"), lax.axis_index("gy"), lax.axis_index("gz")
    core, yc = lax.rem(y, 2), lax.div(y, 2)

    def there(dx, dy, f):
        flip = 1 - core if f else core
        return lax.rem(x + dx + GX, GX), 2 * lax.rem(yc + dy + YC, YC) + flip

    def dev(dx, dy, f):
        return (*there(dx, dy, f), z)

    def hops(dx, dy):
        return min(dx, GX - dx) + min(dy, YC - dy)

    offsets = [(dx, dy, f) for dx in range(GX) for dy in range(YC) for f in range(2) if dx or dy or f]
    near = sorted((o for o in offsets if hops(*o[:2]) <= 2), key=lambda o: -hops(*o[:2]))
    far = sorted((o for o in offsets if hops(*o[:2]) > 2), key=lambda o: -hops(*o[:2]))
    corners = [dev(1, 1, 0), dev(3, 3, 0)]
    barrier = pltpu.get_barrier_semaphore()
    for o in near:
        pl.semaphore_signal(barrier, inc=1, device_id=dev(*o), device_id_type=MESH)
    perm[...] = swap16()

    for j in range(16):
        cols = slice(j * 256, (j + 1) * 256)
        t[:, cols] = jnp.dot(factor_t[...], xs[:, cols], preferred_element_type=jnp.float32).astype(jnp.bfloat16)
    for r0 in range(0, 128, 16):
        halves = [
            jnp.concatenate([t[r0:r0 + 16, h + j * 128:h + (j + 1) * 128] for j in range(16)], axis=0) for h in (0, 2048)
        ]
        block = jnp.concatenate(halves, axis=1)
        rows = jnp.dot(perm[...], block, preferred_element_type=jnp.float32).astype(jnp.bfloat16)
        buf[r0:r0 + 16] = rows.reshape(16, 16, 256)
    pl.semaphore_wait(barrier, len(near))
    for corner in corners:
        pl.semaphore_signal(ready, inc=1, device_id=corner, device_id_type=MESH)

    def place(px, py):
        return out.at[:, pl.ds(pl.multiple_of(py * 64 + px * 16, 16), 16), :]

    def number(dx, dy, f):
        return (dx * YC + dy) * 2 + f

    copies = []

    def push(o):
        px, py = there(*o)
        src = buf.at[pl.ds(px * 32 + py * 4, 4)]
        copies.append(remote(src, place(x, y), send.at[number(*o)], recv.at[number(*o)], dev(*o)))
        copies[-1].start()

    two = [o for o in near if hops(*o[:2]) == 2]
    for o in two:
        push(o)
    pl.semaphore_wait(ready, len(corners))
    for o in far + near[len(two):]:
        push(o)
    mine = pltpu.make_async_copy(buf.at[pl.ds(x * 32 + y * 4, 4)], place(x, y), own_sem)
    mine.start()
    for c in copies:
        c.wait_send()
    for dx, dy, f in near + far:
        at = place(*there(-dx, -dy, f))
        n = number(dx, dy, f)
        remote(at, at, send.at[n], recv.at[n], dev(dx, dy, f)).wait_recv()
    mine.wait()


def split3(q):
    a = q.astype(jnp.bfloat16).astype(jnp.float32)
    b = (q - a).astype(jnp.bfloat16).astype(jnp.float32)
    return a, b, q - a - b


def total_of(terms):
    while len(terms) > 1:
        terms = [terms[i] + terms[i + 1] if i + 1 < len(terms) else terms[i] for i in range(0, len(terms), 2)]
    return terms[0]


def inverse_cholesky(a, d):
    lane = lax.broadcasted_iota(jnp.int32, (8, 128), 1)
    sub = lax.broadcasted_iota(jnp.int32, (8, 128), 0)

    def repeat(v, l):
        return jnp.broadcast_to(v[:, l:l + 1], (8, 128))

    rows = [jnp.broadcast_to(a[i:i + 1, :], (8, 128)) for i in range(8)]
    for base in range(0, 128, 8):
        inside = (lane >= base) & (lane < base + 8)
        s = [[repeat(rows[i], base + k) for k in range(i + 1)] for i in range(8)]
        w = [jnp.where(inside, jnp.where(lane == base + i, 1.0, 0.0), rows[i]) for i in range(8)]
        inverse = []
        for k in range(8):
            inverse.append(1.0 / s[k][k])
            for i in range(k + 1, 8):
                m = s[i][k] * inverse[k]
                for l in range(k + 1, i + 1):
                    s[i][l] = s[i][l] - m * s[l][k]
                w[i] = w[i] - m * w[k]
        p, scale, pivot = w[0], inverse[0], s[0][0]
        for i in range(1, 8):
            p = jnp.where(sub == i, w[i], p)
            scale = jnp.where(sub == i, inverse[i], scale)
            pivot = jnp.where(sub == i, s[i][i], pivot)
        a[base:base + 8, :] = p
        d[base:base + 8, :] = pivot
        now, after = base + 8, base + 16
        if now < 128:
            before = [jnp.broadcast_to(a[now + i:now + i + 1, :], (8, 128)) for i in range(8)]
            rows = [
                jnp.where(inside, 0.0, before[i])
                - total_of([repeat(w[k], now + i) * inverse[k] * w[k] for k in range(8)])
                for i in range(8)
            ]
        if after < 128:
            u, v = split3(p), split3(p * scale)
            left = jnp.concatenate([u[0], u[0], u[1], u[0], u[1], u[2]], axis=0).astype(jnp.bfloat16)
            right = jnp.concatenate([v[0], v[1], v[0], v[2], v[1], v[0]], axis=0).astype(jnp.bfloat16)
            change = lax.dot_general(left, right, (((0,), (0,)), ((), ())), preferred_element_type=jnp.float32)
            old = a[after:, :]
            a[after:, :] = jnp.where(jnp.broadcast_to(inside[:1], old.shape), 0.0, old) - change[after:, :]


def exact_dot(u, v, dims=((1,), (0,))):
    return lax.dot_general(u, v, (dims, ((), ())), precision=lax.Precision.HIGHEST, preferred_element_type=jnp.float32)


def factor_kernel(packed, sketch, factor, factor_t, gram, basis, image, a, d, diagonal):
    row = lax.broadcasted_iota(jnp.int32, (128, 128), 0)
    col = lax.broadcasted_iota(jnp.int32, (128, 128), 1)

    def put(r, c, block):
        gram[128 * r:128 * r + 128, 128 * c:128 * c + 128] = block
        if r < c:
            gram[128 * c:128 * c + 128, 128 * r:128 * r + 128] = block.T

    for c in range(3):
        for r in range(c + 1):
            put(r, c, packed[FIRST[c] + 128 * r:FIRST[c] + 128 * r + 128, :])
    third = packed[FIRST[3]:FIRST[3] + 224, :]
    third = jnp.concatenate([third[:, :64], third[:, 64:], jnp.zeros((64, 64), jnp.float32)], axis=0)
    fourth = packed[FIRST[4]:FIRST[4] + 256, :]
    fourth = jnp.concatenate([fourth[:, :64], fourth[:, 64:]], axis=0)
    panel = jnp.concatenate([third, fourth], axis=1)
    for r in range(3):
        put(r, 3, panel[128 * r:128 * r + 128, :])
    corner = panel[384:512, :]
    put(3, 3, jnp.where((row >= 64) & (col < 64), corner.T, corner))
    order = [(128 * b + START[k], BASE[k] + b * LENGTH[k], LENGTH[k]) for k in range(len(LENGTH)) for b in range(GX)]
    start = jnp.concatenate([sketch[at:at + n, :] for at, _, n in order], axis=0).T
    def orthonormalize():
        inner = exact_dot(image[...], image[...], ((1,), (1,)))
        a[...] = inner
        diagonal[...] = jnp.where(row == col, inner, 0.0)
        inverse_cholesky(a, d)
        lower = jnp.where(col <= row, a[...] * lax.rsqrt(d[...]), 0.0)
        basis[...] = exact_dot(lower, image[...])

    def finish():
        factor_t[...] = basis[...].astype(jnp.bfloat16)
        final = basis[...].T
        for at, place, n in order:
            factor[at:at + n, :] = final[place:place + n, :]

    first = exact_dot(start, gram[...])
    first = first * lax.rsqrt(jnp.sum(first * first, axis=1, keepdims=True))
    image[...] = exact_dot(first, gram[...])
    orthonormalize()
    finish()
    kept = jnp.where(row == col, d[...], 1.0) >= 1e-3 * diagonal[...]
    small = jnp.sum(jnp.where(kept, 0.0, 1.0))

    @pl.when(small > 0.0)
    def _():
        basis[...] = start

        def sweep(step, carry):
            image[...] = exact_dot(basis[...], gram[...])
            orthonormalize()
            return carry

        lax.fori_loop(0, ITERS, sweep, 0)
        finish()


VMEM = pl.BlockSpec(memory_space=pltpu.VMEM)
ANY = pl.BlockSpec(memory_space=pl.ANY)
DMA = pltpu.SemaphoreType.DMA


def shards(field, sketch):
    xs, packed = pl.pallas_call(
        gram_kernel,
        out_shape=(
            jax.ShapeDtypeStruct((512, 4096), jnp.bfloat16),
            jax.ShapeDtypeStruct((1280, 128), jnp.float32),
        ),
        in_specs=[pl.BlockSpec(memory_space=pltpu.HBM)],
        out_specs=(VMEM, VMEM),
        scratch_shapes=[
            pltpu.VMEM((GX, 128, 16, 256), jnp.bfloat16),
            pltpu.VMEM((256, 256), jnp.bfloat16),
            pltpu.VMEM((1280, 128), jnp.float32),
            pltpu.VMEM((640, 128), jnp.float32),
            pltpu.VMEM((640, 128), jnp.float32),
            pltpu.VMEM((PLANE, 24, 128), jnp.float32),
            pltpu.VMEM((PLANE, 16, 128), jnp.float32),
            pltpu.VMEM((GZ, 24, 128), jnp.float32),
            pltpu.VMEM((GZ, 16, 128), jnp.float32),
            DMA((GX * len(PARTS),)), DMA((GX * len(PARTS),)), DMA,
            DMA((2,)), DMA((2,)),
            DMA((2, PLANE)), DMA((2, PLANE)),
            DMA((2, GZ)), DMA((2, GZ)),
            DMA((2, PLANE)), DMA((2, PLANE)),
            DMA((2, GX)), DMA((2, GX)),
        ],
        compiler_params=pltpu.CompilerParams(
            collective_id=0, has_side_effects=True, vmem_limit_bytes=24 * 2**20
        ),
        name="gram",
    )(pltpu.with_memory_space_constraint(field, pltpu.HBM))
    factor, factor_t = pl.pallas_call(
        factor_kernel,
        out_shape=(
            jax.ShapeDtypeStruct((512, 128), jnp.float32),
            jax.ShapeDtypeStruct((128, 512), jnp.bfloat16),
        ),
        in_specs=[VMEM, VMEM],
        out_specs=(VMEM, VMEM),
        scratch_shapes=[
            pltpu.VMEM((512, 512), jnp.float32),
            pltpu.VMEM((128, 512), jnp.float32),
            pltpu.VMEM((128, 512), jnp.float32),
            pltpu.VMEM((128, 128), jnp.float32),
            pltpu.VMEM((128, 128), jnp.float32),
            pltpu.VMEM((128, 128), jnp.float32),
        ],
        compiler_params=pltpu.CompilerParams(vmem_limit_bytes=16 * 2**20),
        name="factor",
    )(packed, sketch)
    core = pl.pallas_call(
        core_kernel,
        out_shape=jax.ShapeDtypeStruct((4, 512, 256), jnp.bfloat16),
        in_specs=[VMEM, VMEM],
        out_specs=VMEM,
        scratch_shapes=[
            pltpu.VMEM((256, 256), jnp.bfloat16),
            pltpu.VMEM((128, 4096), jnp.bfloat16),
            pltpu.VMEM((128, 16, 256), jnp.bfloat16),
            DMA((GX * GY,)), DMA((GX * GY,)), DMA,
            pltpu.SemaphoreType.REGULAR,
        ],
        compiler_params=pltpu.CompilerParams(
            collective_id=1, has_side_effects=True, vmem_limit_bytes=20 * 2**20
        ),
        name="core",
    )(factor_t, xs)
    return (factor, core)


def solution(mesh):
    return jax.shard_map(
        shards,
        mesh=mesh,
        in_specs=(P("gx", "gy", "gz"), P()),
        out_specs=(P(), P(("gx", "gy"), None, "gz")),
        check_vma=False,
    )
```

```python
import functools

import jax
import jax.numpy as jnp
from jax import lax
from jax.experimental import pallas as pl
from jax.experimental.pallas import tpu as pltpu
from jax.sharding import PartitionSpec as P

ITERS = 2
MESH = pl.DeviceIdType.MESH
GX, GY, GZ = 4, 8, 8
YC = GY // 2
PLANE = GX * YC
LENGTH = (32, 32, 32, 16, 16)
START = (0, 32, 64, 96, 112)
BASE = (0, 128, 256, 384, 448)
LAST = 4
FIRST = (0, 128, 384, 768, 1024)
PARTS = ((0, (0, 1)), (1, (0, 1)), (2, (0, 1)), (3, (0, 1)), (4, (0,)), (4, (1,)))
AHEAD = 3


def remote(src, dst, send, recv, dev):
    return pltpu.make_async_remote_copy(
        src_ref=src, dst_ref=dst, send_sem=send, recv_sem=recv,
        device_id=dev, device_id_type=MESH,
    )


def swap16():
    row = lax.broadcasted_iota(jnp.int32, (256, 256), 0)
    col = lax.broadcasted_iota(jnp.int32, (256, 256), 1)
    hit = ((row & 15) * 16 + (row >> 4)) == col
    return jnp.where(hit, 1.0, 0.0).astype(jnp.bfloat16)


def gram_kernel(field, xs, gfin, raw, perm, gp, got, acc, r2e, r2l, r3e, r3l, a_send, a_recv, own_sem,
                c_send, c_recv, p_send, p_recv, z_send, z_recv, g_send, g_recv, f_send, f_recv):
    x, y, z = lax.axis_index("gx"), lax.axis_index("gy"), lax.axis_index("gz")
    core, yc = lax.rem(y, 2), lax.div(y, 2)
    other = (x, y + 1 - 2 * core, z)

    def xdev(d):
        return (lax.rem(x + d, GX), y, z)

    def zdev(d):
        return (x, y, lax.rem(z + d, GZ))

    def pdev(d):
        return (lax.rem(x + d // YC, GX), 2 * lax.rem(yc + d % YC, YC) + core, z)

    def pnum(d):
        return lax.rem(x + d // YC + GX, GX) * YC + lax.rem(yc + d % YC, YC)

    def pfrom(d):
        return lax.rem(x - d // YC + GX, GX) * YC + lax.rem(yc - d % YC + YC, YC)

    barrier = pltpu.get_barrier_semaphore()
    peers = [pdev(d) for d in (8, 4, 12, 10, 2, 6, 9, 11, 14, 1, 3, 5, 7, 13, 15)] + [zdev(d) for d in (4, 3, 5, 2, 6, 1, 7)]
    for dev in peers + [other]:
        pl.semaphore_signal(barrier, inc=1, device_id=dev, device_id_type=MESH)

    pieces = 16
    pl.semaphore_wait(barrier, len(peers) + 1)

    sends = {}
    for m, (k, halves) in enumerate(PARTS):
        rows = pl.ds(START[k], LENGTH[k])
        cols = pl.ds(halves[0] * 128, len(halves) * 128)
        for d in (2, 1, 3):
            to = lax.rem(x + d, GX)
            sends[d, m] = remote(
                field.at[rows, pl.ds(pl.multiple_of(to * pieces, pieces), pieces), cols],
                raw.at[GX - d, rows, :, cols],
                a_send.at[d * len(PARTS) + m], a_recv.at[(GX - d) * len(PARTS) + m], xdev(d),
            )
            if m < AHEAD:
                sends[d, m].start()
    mine = pltpu.make_async_copy(
        field.at[:, pl.ds(pl.multiple_of(x * pieces, pieces), pieces), :], raw.at[0], own_sem
    )
    mine.start()
    perm[...] = swap16()

    def relayout(d, m):
        k, halves = PARTS[m]
        base = BASE[k] + lax.rem(x + d, GX) * LENGTH[k]
        for g in range(0, LENGTH[k], 16):
            block = raw[d, START[k] + g:START[k] + g + 16, :, halves[0] * 128:halves[-1] * 128 + 128]
            block = block.reshape(256, 128 * len(halves))
            out = jnp.dot(perm[...], block, preferred_element_type=jnp.float32).astype(jnp.bfloat16)
            for n, h in enumerate(halves):
                for j in range(16):
                    xs[pl.ds(pl.multiple_of(base + g, 16), 16), h * 2048 + j * 128:h * 2048 + j * 128 + 128] = (
                        out[j * 16:(j + 1) * 16, n * 128:(n + 1) * 128]
                    )

    left_lanes = lax.broadcasted_iota(jnp.int32, (1, 128), 1) < 64

    def products(m):
        k, halves = PARTS[m]
        wide = 4 * LENGTH[k]
        n = BASE[k] + wide
        for step in range(2 * halves[0], 2 * halves[-1] + 2):
            cols = slice(step * 1024, (step + 1) * 1024)
            right = xs[BASE[k]:n, cols]
            if wide == 64:
                right = jnp.concatenate([right, right], axis=0)
            part = lax.dot_general(
                xs[0:n, cols], right, (((1,), (1,)), ((), ())), preferred_element_type=jnp.float32
            )
            if wide == 64:
                part = jnp.where(left_lanes, part[:n // 2], part[n // 2:])
            at = slice(FIRST[k], FIRST[k] + part.shape[0])
            gp[at, :] = part if step == 0 else gp[at, :] + part

    me = pnum(0)
    order = [10, 2, 8, 6, 9, 11, 14, 1, 3, 4, 12, 5, 7, 13, 15]
    pending = []

    def start(copy):
        copy.start()
        pending.append(copy)
        return copy

    def settle():
        while pending:
            pending.pop(0).wait_send()

    class Sum:
        def __init__(self, n, lo, size, r2, r3):
            self.n, self.lo, self.half, self.piece = n, lo, size // 2, size // 2 // PLANE
            self.r2, self.r3 = r2, r3

        def mine(self, which, q=0, size=None):
            first = self.lo + which * self.half + q * self.piece
            return pl.ds(pl.multiple_of(first, 8), self.half if size is None else size)

        def to_core(self):
            self.swap = start(remote(
                gp.at[self.mine(1 - core)], got.at[pl.ds(self.lo // 2, self.half)],
                c_send.at[self.n], c_recv.at[self.n], other,
            ))

        def from_core(self):
            self.swap.wait_recv()
            here = slice(self.lo // 2, self.lo // 2 + self.half)
            acc[here] = gp[self.mine(core)] + got[here]

        def part(self, q):
            return pl.ds(pl.multiple_of(self.lo // 2 + q * self.piece, 8), self.piece)

        def to_plane(self):
            for d in order:
                start(remote(acc.at[self.part(pnum(d))], self.r2.at[me], p_send.at[self.n, d], p_recv.at[self.n, d], pdev(d)))
            self.r2[me] = acc[self.part(me)]

        def from_plane(self):
            for d in order:
                at = self.r2.at[pfrom(d)]
                remote(at, at, p_send.at[self.n, d], p_recv.at[self.n, d], pdev(d)).wait_recv()
            self.r3[z] = total_of([self.r2[q] for q in range(PLANE)])

        def to_line(self):
            for d in (4, 3, 5, 2, 6, 1, 7):
                start(remote(self.r3.at[z], self.r3.at[z], z_send.at[self.n, d], z_recv.at[self.n, d], zdev(d)))

        def from_line(self):
            for d in (1, 7, 2, 6, 3, 5, 4):
                at = self.r3.at[lax.rem(z - d + GZ, GZ)]
                remote(at, at, z_send.at[self.n, d], z_recv.at[self.n, d], zdev(d)).wait_recv()
            gfin[self.mine(core, me, self.piece)] = total_of([self.r3[q] for q in range(GZ)])

        def place(self, which, q):
            return gfin.at[self.mine(which, q, self.piece)]

        def spread(self):
            at = self.place(core, me)
            for d in order:
                start(remote(at, at, g_send.at[self.n, d], g_recv.at[self.n, d], pdev(d)))

        def row(self, which, dx):
            first = self.lo + which * self.half + lax.rem(x - dx + GX, GX) * YC * self.piece
            return gfin.at[pl.ds(pl.multiple_of(first, 8), YC * self.piece)]

        def gather(self):
            for dx in (0, 1, 3, 2):
                for dy in range(YC):
                    d = dx * YC + dy
                    if d:
                        at = self.place(core, pfrom(d))
                        remote(at, at, g_send.at[self.n, d], g_recv.at[self.n, d], pdev(d)).wait_recv()
                at = self.row(core, dx)
                start(remote(at, at, f_send.at[self.n, dx], f_recv.at[self.n, dx], other))

        def finish(self):
            for dx in (0, 1, 3, 2):
                at = self.row(1 - core, dx)
                remote(at, at, f_send.at[self.n, dx], f_recv.at[self.n, dx], other).wait_recv()

    early, late = Sum(0, 0, 768, r2e, r3e), Sum(1, 768, 512, r2l, r3l)
    gp[992:1024, :] = jnp.zeros((32, 128), jnp.float32)

    mine.wait()
    for m in range(len(PARTS)):
        relayout(0, m)
    for m in range(len(PARTS)):
        for d in (1, 3, 2):
            sends[GX - d, m].wait_recv()
            if m + AHEAD < len(PARTS):
                sends[GX - d, m + AHEAD].start()
            relayout(d, m)
        products(m)
        if m == 2:
            early.to_core()
            early.from_core()
            early.to_plane()
    late.to_core()
    late.from_core()
    late.to_plane()
    early.from_plane()
    early.to_line()
    late.from_plane()
    late.to_line()
    early.from_line()
    early.spread()
    for c in sends.values():
        c.wait_send()
    settle()
    late.from_line()
    late.spread()
    early.gather()
    early.finish()
    settle()
    late.gather()
    settle()
    late.finish()


def core_kernel(factor_t, xs, out, perm, t, buf, send, recv, own_sem, ready):
    x, y, z = lax.axis_index("gx"), lax.axis_index("gy"), lax.axis_index("gz")
    core, yc = lax.rem(y, 2), lax.div(y, 2)

    def there(dx, dy, f):
        flip = 1 - core if f else core
        return lax.rem(x + dx + GX, GX), 2 * lax.rem(yc + dy + YC, YC) + flip

    def dev(dx, dy, f):
        return (*there(dx, dy, f), z)

    def hops(dx, dy):
        return min(dx, GX - dx) + min(dy, YC - dy)

    offsets = [(dx, dy, f) for dx in range(GX) for dy in range(YC) for f in range(2) if dx or dy or f]
    ring = [sorted((o for o in offsets if hops(*o[:2]) == n), key=lambda o: o[2]) for n in range(5)]
    near, two, far = ring[1] + ring[0], ring[2], ring[4] + ring[3]
    sides = [dev(1, 0, 0), dev(3, 0, 0), dev(0, 1, 0), dev(0, 3, 0)]
    corners = [dev(1, 1, 0), dev(3, 3, 0)]
    barrier = pltpu.get_barrier_semaphore()
    for o in near:
        pl.semaphore_signal(barrier, inc=1, device_id=dev(*o), device_id_type=MESH)
    perm[...] = swap16()

    for j in range(16):
        cols = slice(j * 256, (j + 1) * 256)
        t[:, cols] = jnp.dot(factor_t[...], xs[:, cols], preferred_element_type=jnp.float32).astype(jnp.bfloat16)
    for r0 in range(0, 128, 16):
        halves = [
            jnp.concatenate([t[r0:r0 + 16, h + j * 128:h + (j + 1) * 128] for j in range(16)], axis=0) for h in (0, 2048)
        ]
        block = jnp.concatenate(halves, axis=1)
        rows = jnp.dot(perm[...], block, preferred_element_type=jnp.float32).astype(jnp.bfloat16)
        buf[r0:r0 + 16] = rows.reshape(16, 16, 256)
    pl.semaphore_wait(barrier, len(near))
    for side in sides:
        pl.semaphore_signal(ready.at[0], inc=1, device_id=side, device_id_type=MESH)

    def place(px, py):
        return out.at[:, pl.ds(pl.multiple_of(py * 64 + px * 16, 16), 16), :]

    def number(dx, dy, f):
        return (dx * YC + dy) * 2 + f

    copies = []

    def push(o):
        px, py = there(*o)
        src = buf.at[pl.ds(px * 32 + py * 4, 4)]
        copies.append(remote(src, place(x, y), send.at[number(*o)], recv.at[number(*o)], dev(*o)))
        copies[-1].start()

    for o in near:
        push(o)
    pl.semaphore_wait(ready.at[0], len(sides))
    for corner in corners:
        pl.semaphore_signal(ready.at[1], inc=1, device_id=corner, device_id_type=MESH)
    for o in two:
        push(o)
    pl.semaphore_wait(ready.at[1], len(corners))
    for o in far:
        push(o)
    mine = pltpu.make_async_copy(buf.at[pl.ds(x * 32 + y * 4, 4)], place(x, y), own_sem)
    mine.start()
    for c in copies:
        c.wait_send()
    for dx, dy, f in near + two + far:
        at = place(*there(-dx, -dy, f))
        n = number(dx, dy, f)
        remote(at, at, send.at[n], recv.at[n], dev(dx, dy, f)).wait_recv()
    mine.wait()


def split3(q):
    a = q.astype(jnp.bfloat16).astype(jnp.float32)
    b = (q - a).astype(jnp.bfloat16).astype(jnp.float32)
    return a, b, q - a - b


def total_of(terms):
    while len(terms) > 1:
        terms = [terms[i] + terms[i + 1] if i + 1 < len(terms) else terms[i] for i in range(0, len(terms), 2)]
    return terms[0]


def inverse_cholesky(a, d):
    lane = lax.broadcasted_iota(jnp.int32, (8, 128), 1)
    sub = lax.broadcasted_iota(jnp.int32, (8, 128), 0)

    def repeat(v, l):
        return jnp.broadcast_to(v[:, l:l + 1], (8, 128))

    rows = [jnp.broadcast_to(a[i:i + 1, :], (8, 128)) for i in range(8)]
    for base in range(0, 128, 8):
        inside = (lane >= base) & (lane < base + 8)
        s = [[repeat(rows[i], base + k) for k in range(i + 1)] for i in range(8)]
        w = [jnp.where(inside, jnp.where(lane == base + i, 1.0, 0.0), rows[i]) for i in range(8)]
        inverse = []
        for k in range(8):
            inverse.append(1.0 / s[k][k])
            for i in range(k + 1, 8):
                m = s[i][k] * inverse[k]
                for l in range(k + 1, i + 1):
                    s[i][l] = s[i][l] - m * s[l][k]
                w[i] = w[i] - m * w[k]
        p, scale, pivot = w[0], inverse[0], s[0][0]
        for i in range(1, 8):
            p = jnp.where(sub == i, w[i], p)
            scale = jnp.where(sub == i, inverse[i], scale)
            pivot = jnp.where(sub == i, s[i][i], pivot)
        a[base:base + 8, :] = p
        d[base:base + 8, :] = pivot
        now, after = base + 8, base + 16
        if now < 128:
            before = [jnp.broadcast_to(a[now + i:now + i + 1, :], (8, 128)) for i in range(8)]
            rows = [
                jnp.where(inside, 0.0, before[i])
                - total_of([repeat(w[k], now + i) * inverse[k] * w[k] for k in range(8)])
                for i in range(8)
            ]
        if after < 128:
            u, v = split3(p), split3(p * scale)
            left = jnp.concatenate([u[0], u[0], u[1], u[0], u[1], u[2]], axis=0).astype(jnp.bfloat16)
            right = jnp.concatenate([v[0], v[1], v[0], v[2], v[1], v[0]], axis=0).astype(jnp.bfloat16)
            change = lax.dot_general(left, right, (((0,), (0,)), ((), ())), preferred_element_type=jnp.float32)
            old = a[after:, :]
            a[after:, :] = jnp.where(jnp.broadcast_to(inside[:1], old.shape), 0.0, old) - change[after:, :]


def exact_dot(u, v, dims=((1,), (0,))):
    return lax.dot_general(u, v, (dims, ((), ())), precision=lax.Precision.HIGHEST, preferred_element_type=jnp.float32)


def factor_kernel(packed, sketch, factor, factor_t, gram, basis, image, a, d, diagonal):
    row = lax.broadcasted_iota(jnp.int32, (128, 128), 0)
    col = lax.broadcasted_iota(jnp.int32, (128, 128), 1)

    def put(r, c, block):
        gram[128 * r:128 * r + 128, 128 * c:128 * c + 128] = block
        if r < c:
            gram[128 * c:128 * c + 128, 128 * r:128 * r + 128] = block.T

    for c in range(3):
        for r in range(c + 1):
            put(r, c, packed[FIRST[c] + 128 * r:FIRST[c] + 128 * r + 128, :])
    third = packed[FIRST[3]:FIRST[3] + 224, :]
    third = jnp.concatenate([third[:, :64], third[:, 64:], jnp.zeros((64, 64), jnp.float32)], axis=0)
    fourth = packed[FIRST[4]:FIRST[4] + 256, :]
    fourth = jnp.concatenate([fourth[:, :64], fourth[:, 64:]], axis=0)
    panel = jnp.concatenate([third, fourth], axis=1)
    for r in range(3):
        put(r, 3, panel[128 * r:128 * r + 128, :])
    corner = panel[384:512, :]
    put(3, 3, jnp.where((row >= 64) & (col < 64), corner.T, corner))
    order = [(128 * b + START[k], BASE[k] + b * LENGTH[k], LENGTH[k]) for k in range(len(LENGTH)) for b in range(GX)]
    start = jnp.concatenate([sketch[at:at + n, :] for at, _, n in order], axis=0).T
    def orthonormalize():
        inner = exact_dot(image[...], image[...], ((1,), (1,)))
        a[...] = inner
        diagonal[...] = jnp.where(row == col, inner, 0.0)
        inverse_cholesky(a, d)
        lower = jnp.where(col <= row, a[...] * lax.rsqrt(d[...]), 0.0)
        basis[...] = exact_dot(lower, image[...])

    def finish():
        factor_t[...] = basis[...].astype(jnp.bfloat16)
        final = basis[...].T
        for at, place, n in order:
            factor[at:at + n, :] = final[place:place + n, :]

    first = exact_dot(start, gram[...])
    first = first * lax.rsqrt(jnp.sum(first * first, axis=1, keepdims=True))
    image[...] = exact_dot(first, gram[...])
    orthonormalize()
    finish()
    kept = jnp.where(row == col, d[...], 1.0) >= 1e-3 * diagonal[...]
    small = jnp.sum(jnp.where(kept, 0.0, 1.0))

    @pl.when(small > 0.0)
    def _():
        basis[...] = start

        def sweep(step, carry):
            image[...] = exact_dot(basis[...], gram[...])
            orthonormalize()
            return carry

        lax.fori_loop(0, ITERS, sweep, 0)
        finish()


VMEM = pl.BlockSpec(memory_space=pltpu.VMEM)
ANY = pl.BlockSpec(memory_space=pl.ANY)
DMA = pltpu.SemaphoreType.DMA


def shards(field, sketch):
    xs, packed = pl.pallas_call(
        gram_kernel,
        out_shape=(
            jax.ShapeDtypeStruct((512, 4096), jnp.bfloat16),
            jax.ShapeDtypeStruct((1280, 128), jnp.float32),
        ),
        in_specs=[pl.BlockSpec(memory_space=pltpu.HBM)],
        out_specs=(VMEM, VMEM),
        scratch_shapes=[
            pltpu.VMEM((GX, 128, 16, 256), jnp.bfloat16),
            pltpu.VMEM((256, 256), jnp.bfloat16),
            pltpu.VMEM((1280, 128), jnp.float32),
            pltpu.VMEM((640, 128), jnp.float32),
            pltpu.VMEM((640, 128), jnp.float32),
            pltpu.VMEM((PLANE, 24, 128), jnp.float32),
            pltpu.VMEM((PLANE, 16, 128), jnp.float32),
            pltpu.VMEM((GZ, 24, 128), jnp.float32),
            pltpu.VMEM((GZ, 16, 128), jnp.float32),
            DMA((GX * len(PARTS),)), DMA((GX * len(PARTS),)), DMA,
            DMA((2,)), DMA((2,)),
            DMA((2, PLANE)), DMA((2, PLANE)),
            DMA((2, GZ)), DMA((2, GZ)),
            DMA((2, PLANE)), DMA((2, PLANE)),
            DMA((2, GX)), DMA((2, GX)),
        ],
        compiler_params=pltpu.CompilerParams(
            collective_id=0, has_side_effects=True, vmem_limit_bytes=24 * 2**20
        ),
        name="gram",
    )(pltpu.with_memory_space_constraint(field, pltpu.HBM))
    factor, factor_t = pl.pallas_call(
        factor_kernel,
        out_shape=(
            jax.ShapeDtypeStruct((512, 128), jnp.float32),
            jax.ShapeDtypeStruct((128, 512), jnp.bfloat16),
        ),
        in_specs=[VMEM, VMEM],
        out_specs=(VMEM, VMEM),
        scratch_shapes=[
            pltpu.VMEM((512, 512), jnp.float32),
            pltpu.VMEM((128, 512), jnp.float32),
            pltpu.VMEM((128, 512), jnp.float32),
            pltpu.VMEM((128, 128), jnp.float32),
            pltpu.VMEM((128, 128), jnp.float32),
            pltpu.VMEM((128, 128), jnp.float32),
        ],
        compiler_params=pltpu.CompilerParams(vmem_limit_bytes=16 * 2**20),
        name="factor",
    )(packed, sketch)
    core = pl.pallas_call(
        core_kernel,
        out_shape=jax.ShapeDtypeStruct((4, 512, 256), jnp.bfloat16),
        in_specs=[VMEM, VMEM],
        out_specs=VMEM,
        scratch_shapes=[
            pltpu.VMEM((256, 256), jnp.bfloat16),
            pltpu.VMEM((128, 4096), jnp.bfloat16),
            pltpu.VMEM((128, 16, 256), jnp.bfloat16),
            DMA((GX * GY,)), DMA((GX * GY,)), DMA,
            pltpu.SemaphoreType.REGULAR((2,)),
        ],
        compiler_params=pltpu.CompilerParams(
            collective_id=1, has_side_effects=True, vmem_limit_bytes=20 * 2**20
        ),
        name="core",
    )(factor_t, xs)
    return (factor, core)


def solution(mesh):
    return jax.shard_map(
        shards,
        mesh=mesh,
        in_specs=(P("gx", "gy", "gz"), P()),
        out_specs=(P(), P(("gx", "gy"), None, "gz")),
        check_vma=False,
    )
```

```python
import functools

import jax
import jax.numpy as jnp
from jax import lax
from jax.experimental import pallas as pl
from jax.experimental.pallas import tpu as pltpu
from jax.sharding import PartitionSpec as P

ITERS = 2
MESH = pl.DeviceIdType.MESH
GX, GY, GZ = 4, 8, 8
YC = GY // 2
PLANE = GX * YC
LENGTH = (32, 32, 32, 16, 16)
START = (0, 32, 64, 96, 112)
BASE = (0, 128, 256, 384, 448)
LAST = 4
FIRST = (0, 128, 384, 768, 1024)
PARTS = ((0, (0, 1)), (1, (0, 1)), (2, (0, 1)), (3, (0, 1)), (4, (0,)), (4, (1,)))
AHEAD = 3
ORDER = [(128 * b + START[k], BASE[k] + b * LENGTH[k], LENGTH[k]) for k in range(len(LENGTH)) for b in range(GX)]


def remote(src, dst, send, recv, dev):
    return pltpu.make_async_remote_copy(
        src_ref=src, dst_ref=dst, send_sem=send, recv_sem=recv,
        device_id=dev, device_id_type=MESH,
    )


def swap16():
    row = lax.broadcasted_iota(jnp.int32, (256, 256), 0)
    col = lax.broadcasted_iota(jnp.int32, (256, 256), 1)
    hit = ((row & 15) * 16 + (row >> 4)) == col
    return jnp.where(hit, 1.0, 0.0).astype(jnp.bfloat16)


def gram_kernel(field, xs, gfin, raw, perm, gp, got, acc, r2e, r2l, r3e, r3l, a_send, a_recv, own_sem,
                c_send, c_recv, p_send, p_recv, z_send, z_recv, g_send, g_recv, f_send, f_recv):
    x, y, z = lax.axis_index("gx"), lax.axis_index("gy"), lax.axis_index("gz")
    core, yc = lax.rem(y, 2), lax.div(y, 2)
    other = (x, y + 1 - 2 * core, z)

    def xdev(d):
        return (lax.rem(x + d, GX), y, z)

    def zdev(d):
        return (x, y, lax.rem(z + d, GZ))

    def pdev(d):
        return (lax.rem(x + d // YC, GX), 2 * lax.rem(yc + d % YC, YC) + core, z)

    def pnum(d):
        return lax.rem(x + d // YC + GX, GX) * YC + lax.rem(yc + d % YC, YC)

    def pfrom(d):
        return lax.rem(x - d // YC + GX, GX) * YC + lax.rem(yc - d % YC + YC, YC)

    barrier = pltpu.get_barrier_semaphore()
    peers = [pdev(d) for d in (8, 4, 12, 10, 2, 6, 9, 11, 14, 1, 3, 5, 7, 13, 15)] + [zdev(d) for d in (4, 3, 5, 2, 6, 1, 7)]
    for dev in peers + [other]:
        pl.semaphore_signal(barrier, inc=1, device_id=dev, device_id_type=MESH)

    pieces = 16
    pl.semaphore_wait(barrier, len(peers) + 1)

    sends = {}
    for m, (k, halves) in enumerate(PARTS):
        rows = pl.ds(START[k], LENGTH[k])
        cols = pl.ds(halves[0] * 128, len(halves) * 128)
        for d in (2, 1, 3):
            to = lax.rem(x + d, GX)
            sends[d, m] = remote(
                field.at[rows, pl.ds(pl.multiple_of(to * pieces, pieces), pieces), cols],
                raw.at[GX - d, rows, :, cols],
                a_send.at[d * len(PARTS) + m], a_recv.at[(GX - d) * len(PARTS) + m], xdev(d),
            )
            if m < AHEAD:
                sends[d, m].start()
    mine = pltpu.make_async_copy(
        field.at[:, pl.ds(pl.multiple_of(x * pieces, pieces), pieces), :], raw.at[0], own_sem
    )
    mine.start()
    perm[...] = swap16()

    def relayout(d, m):
        k, halves = PARTS[m]
        base = BASE[k] + lax.rem(x + d, GX) * LENGTH[k]
        for g in range(0, LENGTH[k], 16):
            block = raw[d, START[k] + g:START[k] + g + 16, :, halves[0] * 128:halves[-1] * 128 + 128]
            block = block.reshape(256, 128 * len(halves))
            out = jnp.dot(perm[...], block, preferred_element_type=jnp.float32).astype(jnp.bfloat16)
            for n, h in enumerate(halves):
                for j in range(16):
                    xs[pl.ds(pl.multiple_of(base + g, 16), 16), h * 2048 + j * 128:h * 2048 + j * 128 + 128] = (
                        out[j * 16:(j + 1) * 16, n * 128:(n + 1) * 128]
                    )

    left_lanes = lax.broadcasted_iota(jnp.int32, (1, 128), 1) < 64

    def products(m):
        k, halves = PARTS[m]
        wide = 4 * LENGTH[k]
        n = BASE[k] + wide
        for step in range(2 * halves[0], 2 * halves[-1] + 2):
            cols = slice(step * 1024, (step + 1) * 1024)
            right = xs[BASE[k]:n, cols]
            if wide == 64:
                right = jnp.concatenate([right, right], axis=0)
            part = lax.dot_general(
                xs[0:n, cols], right, (((1,), (1,)), ((), ())), preferred_element_type=jnp.float32
            )
            if wide == 64:
                part = jnp.where(left_lanes, part[:n // 2], part[n // 2:])
            at = slice(FIRST[k], FIRST[k] + part.shape[0])
            gp[at, :] = part if step == 0 else gp[at, :] + part

    me = pnum(0)
    order = [10, 2, 8, 6, 9, 11, 14, 1, 3, 4, 12, 5, 7, 13, 15]
    pending = []

    def start(copy):
        copy.start()
        pending.append(copy)
        return copy

    def settle():
        while pending:
            pending.pop(0).wait_send()

    class Sum:
        def __init__(self, n, lo, size, r2, r3):
            self.n, self.lo, self.half, self.piece = n, lo, size // 2, size // 2 // PLANE
            self.r2, self.r3 = r2, r3

        def mine(self, which, q=0, size=None):
            first = self.lo + which * self.half + q * self.piece
            return pl.ds(pl.multiple_of(first, 8), self.half if size is None else size)

        def to_core(self):
            self.swap = start(remote(
                gp.at[self.mine(1 - core)], got.at[pl.ds(self.lo // 2, self.half)],
                c_send.at[self.n], c_recv.at[self.n], other,
            ))

        def from_core(self):
            self.swap.wait_recv()
            here = slice(self.lo // 2, self.lo // 2 + self.half)
            acc[here] = gp[self.mine(core)] + got[here]

        def part(self, q):
            return pl.ds(pl.multiple_of(self.lo // 2 + q * self.piece, 8), self.piece)

        def to_plane(self):
            for d in order:
                start(remote(acc.at[self.part(pnum(d))], self.r2.at[me], p_send.at[self.n, d], p_recv.at[self.n, d], pdev(d)))
            self.r2[me] = acc[self.part(me)]

        def from_plane(self):
            for d in order:
                at = self.r2.at[pfrom(d)]
                remote(at, at, p_send.at[self.n, d], p_recv.at[self.n, d], pdev(d)).wait_recv()
            self.r3[z] = total_of([self.r2[q] for q in range(PLANE)])

        def to_line(self):
            for d in (4, 3, 5, 2, 6, 1, 7):
                start(remote(self.r3.at[z], self.r3.at[z], z_send.at[self.n, d], z_recv.at[self.n, d], zdev(d)))

        def from_line(self):
            for d in (1, 7, 2, 6, 3, 5, 4):
                at = self.r3.at[lax.rem(z - d + GZ, GZ)]
                remote(at, at, z_send.at[self.n, d], z_recv.at[self.n, d], zdev(d)).wait_recv()
            gfin[self.mine(core, me, self.piece)] = total_of([self.r3[q] for q in range(GZ)])

        def place(self, which, q):
            return gfin.at[self.mine(which, q, self.piece)]

        def spread(self):
            at = self.place(core, me)
            for d in order:
                start(remote(at, at, g_send.at[self.n, d], g_recv.at[self.n, d], pdev(d)))

        def row(self, which, dx):
            first = self.lo + which * self.half + lax.rem(x - dx + GX, GX) * YC * self.piece
            return gfin.at[pl.ds(pl.multiple_of(first, 8), YC * self.piece)]

        def gather(self):
            for dx in (0, 1, 3, 2):
                for dy in range(YC):
                    d = dx * YC + dy
                    if d:
                        at = self.place(core, pfrom(d))
                        remote(at, at, g_send.at[self.n, d], g_recv.at[self.n, d], pdev(d)).wait_recv()
                at = self.row(core, dx)
                start(remote(at, at, f_send.at[self.n, dx], f_recv.at[self.n, dx], other))

        def finish(self):
            for dx in (0, 1, 3, 2):
                at = self.row(1 - core, dx)
                remote(at, at, f_send.at[self.n, dx], f_recv.at[self.n, dx], other).wait_recv()

    early, late = Sum(0, 0, 768, r2e, r3e), Sum(1, 768, 512, r2l, r3l)
    gp[992:1024, :] = jnp.zeros((32, 128), jnp.float32)

    mine.wait()
    for m in range(len(PARTS)):
        relayout(0, m)
    for m in range(len(PARTS)):
        for d in (1, 3, 2):
            sends[GX - d, m].wait_recv()
            if m + AHEAD < len(PARTS):
                sends[GX - d, m + AHEAD].start()
            relayout(d, m)
        products(m)
        if m == 2:
            early.to_core()
            early.from_core()
            early.to_plane()
    late.to_core()
    late.from_core()
    late.to_plane()
    early.from_plane()
    early.to_line()
    late.from_plane()
    late.to_line()
    early.from_line()
    early.spread()
    for c in sends.values():
        c.wait_send()
    settle()
    late.from_line()
    late.spread()
    early.gather()
    early.finish()
    settle()
    late.gather()
    settle()
    late.finish()


def core_kernel(factor_t, xs, out, perm, t, buf, send, recv, own_sem, ready):
    x, y, z = lax.axis_index("gx"), lax.axis_index("gy"), lax.axis_index("gz")
    core, yc = lax.rem(y, 2), lax.div(y, 2)

    def there(dx, dy, f):
        flip = 1 - core if f else core
        return lax.rem(x + dx + GX, GX), 2 * lax.rem(yc + dy + YC, YC) + flip

    def dev(dx, dy, f):
        return (*there(dx, dy, f), z)

    def hops(dx, dy):
        return min(dx, GX - dx) + min(dy, YC - dy)

    offsets = [(dx, dy, f) for dx in range(GX) for dy in range(YC) for f in range(2) if dx or dy or f]
    ring = [sorted((o for o in offsets if hops(*o[:2]) == n), key=lambda o: o[2]) for n in range(5)]
    near, two, far = ring[1] + ring[0], ring[2], ring[4] + ring[3]
    sides = [dev(1, 0, 0), dev(3, 0, 0), dev(0, 1, 0), dev(0, 3, 0)]
    corners = [dev(1, 1, 0), dev(3, 3, 0)]
    barrier = pltpu.get_barrier_semaphore()
    for o in near:
        pl.semaphore_signal(barrier, inc=1, device_id=dev(*o), device_id_type=MESH)
    perm[...] = swap16()

    for j in range(16):
        cols = slice(j * 256, (j + 1) * 256)
        t[:, cols] = jnp.dot(factor_t[...], xs[:, cols], preferred_element_type=jnp.float32).astype(jnp.bfloat16)
    for r0 in range(0, 128, 16):
        halves = [
            jnp.concatenate([t[r0:r0 + 16, h + j * 128:h + (j + 1) * 128] for j in range(16)], axis=0) for h in (0, 2048)
        ]
        block = jnp.concatenate(halves, axis=1)
        rows = jnp.dot(perm[...], block, preferred_element_type=jnp.float32).astype(jnp.bfloat16)
        buf[r0:r0 + 16] = rows.reshape(16, 16, 256)
    pl.semaphore_wait(barrier, len(near))
    for side in sides:
        pl.semaphore_signal(ready.at[0], inc=1, device_id=side, device_id_type=MESH)

    def place(px, py):
        return out.at[:, pl.ds(pl.multiple_of(py * 64 + px * 16, 16), 16), :]

    def number(dx, dy, f):
        return (dx * YC + dy) * 2 + f

    copies = []

    def push(o):
        px, py = there(*o)
        src = buf.at[pl.ds(px * 32 + py * 4, 4)]
        copies.append(remote(src, place(x, y), send.at[number(*o)], recv.at[number(*o)], dev(*o)))
        copies[-1].start()

    for o in near:
        push(o)
    pl.semaphore_wait(ready.at[0], len(sides))
    for corner in corners:
        pl.semaphore_signal(ready.at[1], inc=1, device_id=corner, device_id_type=MESH)
    for o in two:
        push(o)
    pl.semaphore_wait(ready.at[1], len(corners))
    for o in far:
        push(o)
    mine = pltpu.make_async_copy(buf.at[pl.ds(x * 32 + y * 4, 4)], place(x, y), own_sem)
    mine.start()
    for c in copies:
        c.wait_send()
    for dx, dy, f in near + two + far:
        at = place(*there(-dx, -dy, f))
        n = number(dx, dy, f)
        remote(at, at, send.at[n], recv.at[n], dev(dx, dy, f)).wait_recv()
    mine.wait()


def split3(q):
    a = q.astype(jnp.bfloat16).astype(jnp.float32)
    b = (q - a).astype(jnp.bfloat16).astype(jnp.float32)
    return a, b, q - a - b


def total_of(terms):
    while len(terms) > 1:
        terms = [terms[i] + terms[i + 1] if i + 1 < len(terms) else terms[i] for i in range(0, len(terms), 2)]
    return terms[0]


def inverse_cholesky(a, d):
    lane = lax.broadcasted_iota(jnp.int32, (8, 128), 1)
    sub = lax.broadcasted_iota(jnp.int32, (8, 128), 0)

    def repeat(v, l):
        return jnp.broadcast_to(v[:, l:l + 1], (8, 128))

    rows = [jnp.broadcast_to(a[i:i + 1, :], (8, 128)) for i in range(8)]
    for base in range(0, 128, 8):
        inside = (lane >= base) & (lane < base + 8)
        s = [[repeat(rows[i], base + k) for k in range(i + 1)] for i in range(8)]
        w = [jnp.where(inside, jnp.where(lane == base + i, 1.0, 0.0), rows[i]) for i in range(8)]
        inverse = []
        for k in range(8):
            inverse.append(1.0 / s[k][k])
            for i in range(k + 1, 8):
                m = s[i][k] * inverse[k]
                for l in range(k + 1, i + 1):
                    s[i][l] = s[i][l] - m * s[l][k]
                w[i] = w[i] - m * w[k]
        p, scale, pivot = w[0], inverse[0], s[0][0]
        for i in range(1, 8):
            p = jnp.where(sub == i, w[i], p)
            scale = jnp.where(sub == i, inverse[i], scale)
            pivot = jnp.where(sub == i, s[i][i], pivot)
        a[base:base + 8, :] = p
        d[base:base + 8, :] = pivot
        now, after = base + 8, base + 16
        if now < 128:
            before = [jnp.broadcast_to(a[now + i:now + i + 1, :], (8, 128)) for i in range(8)]
            rows = [
                jnp.where(inside, 0.0, before[i])
                - total_of([repeat(w[k], now + i) * inverse[k] * w[k] for k in range(8)])
                for i in range(8)
            ]
        if after < 128:
            u, v = split3(p), split3(p * scale)
            left = jnp.concatenate([u[0], u[0], u[1], u[0], u[1], u[2]], axis=0).astype(jnp.bfloat16)
            right = jnp.concatenate([v[0], v[1], v[0], v[2], v[1], v[0]], axis=0).astype(jnp.bfloat16)
            change = lax.dot_general(left, right, (((0,), (0,)), ((), ())), preferred_element_type=jnp.float32)
            old = a[after:, :]
            a[after:, :] = jnp.where(jnp.broadcast_to(inside[:1], old.shape), 0.0, old) - change[after:, :]


def exact_dot(u, v, dims=((1,), (0,))):
    return lax.dot_general(u, v, (dims, ((), ())), precision=lax.Precision.HIGHEST, preferred_element_type=jnp.float32)


def factor_kernel(packed, sketch, basis, factor_t, gram, image, a, d, diagonal):
    row = lax.broadcasted_iota(jnp.int32, (128, 128), 0)
    col = lax.broadcasted_iota(jnp.int32, (128, 128), 1)

    def put(r, c, block):
        gram[128 * r:128 * r + 128, 128 * c:128 * c + 128] = block
        if r < c:
            gram[128 * c:128 * c + 128, 128 * r:128 * r + 128] = block.T

    for c in range(3):
        for r in range(c + 1):
            put(r, c, packed[FIRST[c] + 128 * r:FIRST[c] + 128 * r + 128, :])
    third = packed[FIRST[3]:FIRST[3] + 224, :]
    third = jnp.concatenate([third[:, :64], third[:, 64:], jnp.zeros((64, 64), jnp.float32)], axis=0)
    fourth = packed[FIRST[4]:FIRST[4] + 256, :]
    fourth = jnp.concatenate([fourth[:, :64], fourth[:, 64:]], axis=0)
    panel = jnp.concatenate([third, fourth], axis=1)
    for r in range(3):
        put(r, 3, panel[128 * r:128 * r + 128, :])
    corner = panel[384:512, :]
    put(3, 3, jnp.where((row >= 64) & (col < 64), corner.T, corner))
    start = jnp.concatenate([sketch[at:at + n, :] for at, _, n in ORDER], axis=0).T
    def orthonormalize():
        inner = exact_dot(image[...], image[...], ((1,), (1,)))
        a[...] = inner
        diagonal[...] = jnp.where(row == col, inner, 0.0)
        inverse_cholesky(a, d)
        lower = jnp.where(col <= row, a[...] * lax.rsqrt(d[...]), 0.0)
        basis[...] = exact_dot(lower, image[...])

    def finish():
        factor_t[...] = basis[...].astype(jnp.bfloat16)

    first = exact_dot(start, gram[...])
    first = first * lax.rsqrt(jnp.sum(first * first, axis=1, keepdims=True))
    image[...] = exact_dot(first, gram[...])
    orthonormalize()
    finish()
    kept = jnp.where(row == col, d[...], 1.0) >= 1e-3 * diagonal[...]
    small = jnp.sum(jnp.where(kept, 0.0, 1.0))

    @pl.when(small > 0.0)
    def _():
        basis[...] = start

        def sweep(step, carry):
            image[...] = exact_dot(basis[...], gram[...])
            orthonormalize()
            return carry

        lax.fori_loop(0, ITERS, sweep, 0)
        finish()


def store_kernel(core, basis, out, factor, rows, sem):
    copies = [pltpu.make_async_copy(core.at[r], out.at[r], sem.at[r]) for r in range(core.shape[0])]
    for c in copies:
        c.start()
    for c in range(4):
        final = basis[:, 128 * c:128 * c + 128].T
        for at, place, n in ORDER:
            if place // 128 == c:
                rows[at:at + n, :] = final[place - 128 * c:place - 128 * c + n, :]
    copies.append(pltpu.make_async_copy(rows, factor, sem.at[4]))
    copies[-1].start()
    for c in copies:
        c.wait()


VMEM = pl.BlockSpec(memory_space=pltpu.VMEM)
ANY = pl.BlockSpec(memory_space=pl.ANY)
DMA = pltpu.SemaphoreType.DMA


def shards(field, sketch):
    xs, packed = pl.pallas_call(
        gram_kernel,
        out_shape=(
            jax.ShapeDtypeStruct((512, 4096), jnp.bfloat16),
            jax.ShapeDtypeStruct((1280, 128), jnp.float32),
        ),
        in_specs=[pl.BlockSpec(memory_space=pltpu.HBM)],
        out_specs=(VMEM, VMEM),
        scratch_shapes=[
            pltpu.VMEM((GX, 128, 16, 256), jnp.bfloat16),
            pltpu.VMEM((256, 256), jnp.bfloat16),
            pltpu.VMEM((1280, 128), jnp.float32),
            pltpu.VMEM((640, 128), jnp.float32),
            pltpu.VMEM((640, 128), jnp.float32),
            pltpu.VMEM((PLANE, 24, 128), jnp.float32),
            pltpu.VMEM((PLANE, 16, 128), jnp.float32),
            pltpu.VMEM((GZ, 24, 128), jnp.float32),
            pltpu.VMEM((GZ, 16, 128), jnp.float32),
            DMA((GX * len(PARTS),)), DMA((GX * len(PARTS),)), DMA,
            DMA((2,)), DMA((2,)),
            DMA((2, PLANE)), DMA((2, PLANE)),
            DMA((2, GZ)), DMA((2, GZ)),
            DMA((2, PLANE)), DMA((2, PLANE)),
            DMA((2, GX)), DMA((2, GX)),
        ],
        compiler_params=pltpu.CompilerParams(
            collective_id=0, has_side_effects=True, vmem_limit_bytes=24 * 2**20
        ),
        name="gram",
    )(pltpu.with_memory_space_constraint(field, pltpu.HBM))
    basis, factor_t = pl.pallas_call(
        factor_kernel,
        out_shape=(
            jax.ShapeDtypeStruct((128, 512), jnp.float32),
            jax.ShapeDtypeStruct((128, 512), jnp.bfloat16),
        ),
        in_specs=[VMEM, VMEM],
        out_specs=(VMEM, VMEM),
        scratch_shapes=[
            pltpu.VMEM((512, 512), jnp.float32),
            pltpu.VMEM((128, 512), jnp.float32),
            pltpu.VMEM((128, 128), jnp.float32),
            pltpu.VMEM((128, 128), jnp.float32),
            pltpu.VMEM((128, 128), jnp.float32),
        ],
        compiler_params=pltpu.CompilerParams(vmem_limit_bytes=16 * 2**20),
        name="factor",
    )(packed, sketch)
    core = pl.pallas_call(
        core_kernel,
        out_shape=jax.ShapeDtypeStruct((4, 512, 256), jnp.bfloat16),
        in_specs=[VMEM, VMEM],
        out_specs=VMEM,
        scratch_shapes=[
            pltpu.VMEM((256, 256), jnp.bfloat16),
            pltpu.VMEM((128, 4096), jnp.bfloat16),
            pltpu.VMEM((128, 16, 256), jnp.bfloat16),
            DMA((GX * GY,)), DMA((GX * GY,)), DMA,
            pltpu.SemaphoreType.REGULAR((2,)),
        ],
        compiler_params=pltpu.CompilerParams(
            collective_id=1, has_side_effects=True, vmem_limit_bytes=20 * 2**20
        ),
        name="core",
    )(factor_t, xs)
    core, factor = pl.pallas_call(
        store_kernel,
        out_shape=(
            jax.ShapeDtypeStruct((4, 512, 256), jnp.bfloat16),
            jax.ShapeDtypeStruct((512, 128), jnp.float32),
        ),
        in_specs=[VMEM, VMEM],
        out_specs=(ANY, ANY),
        scratch_shapes=[pltpu.VMEM((512, 128), jnp.float32), DMA((5,))],
        compiler_params=pltpu.CompilerParams(vmem_limit_bytes=16 * 2**20),
        name="store",
    )(core, basis)
    return (factor, core)


def solution(mesh):
    return jax.shard_map(
        shards,
        mesh=mesh,
        in_specs=(P("gx", "gy", "gz"), P()),
        out_specs=(P(), P(("gx", "gy"), None, "gz")),
        check_vma=False,
    )
```

```python
import functools

import jax
import jax.numpy as jnp
from jax import lax
from jax.experimental import pallas as pl
from jax.experimental.pallas import tpu as pltpu
from jax.sharding import PartitionSpec as P

ITERS = 2
MESH = pl.DeviceIdType.MESH
GX, GY, GZ = 4, 8, 8
YC = GY // 2
PLANE = GX * YC
LENGTH = (32, 32, 32, 16, 16)
START = (0, 32, 64, 96, 112)
BASE = (0, 128, 256, 384, 448)
LAST = 4
FIRST = (0, 128, 384, 768, 1024)
PARTS = ((0, (0, 1)), (1, (0, 1)), (2, (0, 1)), (3, (0, 1)), (4, (0,)), (4, (1,)))
AHEAD = 3
ORDER = [(128 * b + START[k], BASE[k] + b * LENGTH[k], LENGTH[k]) for k in range(len(LENGTH)) for b in range(GX)]


def remote(src, dst, send, recv, dev):
    return pltpu.make_async_remote_copy(
        src_ref=src, dst_ref=dst, send_sem=send, recv_sem=recv,
        device_id=dev, device_id_type=MESH,
    )


def swap16():
    row = lax.broadcasted_iota(jnp.int32, (256, 256), 0)
    col = lax.broadcasted_iota(jnp.int32, (256, 256), 1)
    hit = ((row & 15) * 16 + (row >> 4)) == col
    return jnp.where(hit, 1.0, 0.0).astype(jnp.bfloat16)


def gram_kernel(field, xs, gfin, raw, perm, gp, got, acc, r2e, r2l, r3e, r3l, a_send, a_recv, own_sem,
                c_send, c_recv, p_send, p_recv, z_send, z_recv, g_send, g_recv, f_send, f_recv):
    x, y, z = lax.axis_index("gx"), lax.axis_index("gy"), lax.axis_index("gz")
    core, yc = lax.rem(y, 2), lax.div(y, 2)
    other = (x, y + 1 - 2 * core, z)

    def xdev(d):
        return (lax.rem(x + d, GX), y, z)

    def zdev(d):
        return (x, y, lax.rem(z + d, GZ))

    def pdev(d):
        return (lax.rem(x + d // YC, GX), 2 * lax.rem(yc + d % YC, YC) + core, z)

    def pnum(d):
        return lax.rem(x + d // YC + GX, GX) * YC + lax.rem(yc + d % YC, YC)

    def pfrom(d):
        return lax.rem(x - d // YC + GX, GX) * YC + lax.rem(yc - d % YC + YC, YC)

    barrier = pltpu.get_barrier_semaphore()
    peers = [pdev(d) for d in (8, 4, 12, 10, 2, 6, 9, 11, 14, 1, 3, 5, 7, 13, 15)] + [zdev(d) for d in (4, 3, 5, 2, 6, 1, 7)]
    for dev in peers + [other]:
        pl.semaphore_signal(barrier, inc=1, device_id=dev, device_id_type=MESH)

    pieces = 16
    pl.semaphore_wait(barrier, len(peers) + 1)

    sends = {}
    for m, (k, halves) in enumerate(PARTS):
        rows = pl.ds(START[k], LENGTH[k])
        cols = pl.ds(halves[0] * 128, len(halves) * 128)
        for d in (2, 1, 3):
            to = lax.rem(x + d, GX)
            sends[d, m] = remote(
                field.at[rows, pl.ds(pl.multiple_of(to * pieces, pieces), pieces), cols],
                raw.at[GX - d, rows, :, cols],
                a_send.at[d * len(PARTS) + m], a_recv.at[(GX - d) * len(PARTS) + m], xdev(d),
            )
            if m < AHEAD:
                sends[d, m].start()
    mine = pltpu.make_async_copy(
        field.at[:, pl.ds(pl.multiple_of(x * pieces, pieces), pieces), :], raw.at[0], own_sem
    )
    mine.start()
    perm[...] = swap16()

    def relayout(d, m):
        k, halves = PARTS[m]
        base = BASE[k] + lax.rem(x + d, GX) * LENGTH[k]
        for g in range(0, LENGTH[k], 16):
            block = raw[d, START[k] + g:START[k] + g + 16, :, halves[0] * 128:halves[-1] * 128 + 128]
            block = block.reshape(256, 128 * len(halves))
            out = jnp.dot(perm[...], block, preferred_element_type=jnp.float32).astype(jnp.bfloat16)
            for n, h in enumerate(halves):
                for j in range(16):
                    xs[pl.ds(pl.multiple_of(base + g, 16), 16), h * 2048 + j * 128:h * 2048 + j * 128 + 128] = (
                        out[j * 16:(j + 1) * 16, n * 128:(n + 1) * 128]
                    )

    left_lanes = lax.broadcasted_iota(jnp.int32, (1, 128), 1) < 64

    def products(m):
        k, halves = PARTS[m]
        wide = 4 * LENGTH[k]
        n = BASE[k] + wide
        for step in range(2 * halves[0], 2 * halves[-1] + 2):
            cols = slice(step * 1024, (step + 1) * 1024)
            right = xs[BASE[k]:n, cols]
            if wide == 64:
                right = jnp.concatenate([right, right], axis=0)
            part = lax.dot_general(
                xs[0:n, cols], right, (((1,), (1,)), ((), ())), preferred_element_type=jnp.float32
            )
            if wide == 64:
                part = jnp.where(left_lanes, part[:n // 2], part[n // 2:])
            at = slice(FIRST[k], FIRST[k] + part.shape[0])
            gp[at, :] = part if step == 0 else gp[at, :] + part

    me = pnum(0)
    order = [10, 2, 8, 6, 9, 11, 14, 1, 3, 4, 12, 5, 7, 13, 15]
    pending = []

    def start(copy):
        copy.start()
        pending.append(copy)
        return copy

    def settle():
        while pending:
            pending.pop(0).wait_send()

    class Sum:
        def __init__(self, n, lo, size, r2, r3):
            self.n, self.lo, self.half, self.piece = n, lo, size // 2, size // 2 // PLANE
            self.r2, self.r3 = r2, r3

        def mine(self, which, q=0, size=None):
            first = self.lo + which * self.half + q * self.piece
            return pl.ds(pl.multiple_of(first, 8), self.half if size is None else size)

        def to_core(self):
            self.swap = start(remote(
                gp.at[self.mine(1 - core)], got.at[pl.ds(self.lo // 2, self.half)],
                c_send.at[self.n], c_recv.at[self.n], other,
            ))

        def from_core(self):
            self.swap.wait_recv()
            here = slice(self.lo // 2, self.lo // 2 + self.half)
            acc[here] = gp[self.mine(core)] + got[here]

        def part(self, q):
            return pl.ds(pl.multiple_of(self.lo // 2 + q * self.piece, 8), self.piece)

        def to_plane(self):
            for d in order:
                start(remote(acc.at[self.part(pnum(d))], self.r2.at[me], p_send.at[self.n, d], p_recv.at[self.n, d], pdev(d)))
            self.r2[me] = acc[self.part(me)]

        def from_plane(self):
            for d in order:
                at = self.r2.at[pfrom(d)]
                remote(at, at, p_send.at[self.n, d], p_recv.at[self.n, d], pdev(d)).wait_recv()
            self.r3[z] = total_of([self.r2[q] for q in range(PLANE)])

        def to_line(self):
            for d in (4, 3, 5, 2, 6, 1, 7):
                start(remote(self.r3.at[z], self.r3.at[z], z_send.at[self.n, d], z_recv.at[self.n, d], zdev(d)))

        def from_line(self):
            for d in (1, 7, 2, 6, 3, 5, 4):
                at = self.r3.at[lax.rem(z - d + GZ, GZ)]
                remote(at, at, z_send.at[self.n, d], z_recv.at[self.n, d], zdev(d)).wait_recv()
            gfin[self.mine(core, me, self.piece)] = total_of([self.r3[q] for q in range(GZ)])

        def place(self, which, q):
            return gfin.at[self.mine(which, q, self.piece)]

        def spread(self):
            at = self.place(core, me)
            for d in order:
                start(remote(at, at, g_send.at[self.n, d], g_recv.at[self.n, d], pdev(d)))

        def row(self, which, dx):
            first = self.lo + which * self.half + lax.rem(x - dx + GX, GX) * YC * self.piece
            return gfin.at[pl.ds(pl.multiple_of(first, 8), YC * self.piece)]

        def gather(self):
            for dx in (0, 1, 3, 2):
                for dy in range(YC):
                    d = dx * YC + dy
                    if d:
                        at = self.place(core, pfrom(d))
                        remote(at, at, g_send.at[self.n, d], g_recv.at[self.n, d], pdev(d)).wait_recv()
                at = self.row(core, dx)
                start(remote(at, at, f_send.at[self.n, dx], f_recv.at[self.n, dx], other))

        def finish(self):
            for dx in (0, 1, 3, 2):
                at = self.row(1 - core, dx)
                remote(at, at, f_send.at[self.n, dx], f_recv.at[self.n, dx], other).wait_recv()

    early, late = Sum(0, 0, 768, r2e, r3e), Sum(1, 768, 512, r2l, r3l)
    gp[992:1024, :] = jnp.zeros((32, 128), jnp.float32)

    mine.wait()
    for m in range(len(PARTS)):
        relayout(0, m)
    for m in range(len(PARTS)):
        for d in (1, 3, 2):
            sends[GX - d, m].wait_recv()
            if m + AHEAD < len(PARTS):
                sends[GX - d, m + AHEAD].start()
            relayout(d, m)
        products(m)
        if m == 2:
            early.to_core()
            early.from_core()
            early.to_plane()
    late.to_core()
    late.from_core()
    late.to_plane()
    early.from_plane()
    early.to_line()
    late.from_plane()
    late.to_line()
    early.from_line()
    early.spread()
    late.from_line()
    late.spread()
    early.gather()
    early.finish()
    for c in sends.values():
        c.wait_send()
    settle()
    late.gather()
    settle()
    late.finish()


def core_kernel(factor_t, xs, out, perm, t, buf, send, recv, own_sem, ready):
    x, y, z = lax.axis_index("gx"), lax.axis_index("gy"), lax.axis_index("gz")
    core, yc = lax.rem(y, 2), lax.div(y, 2)

    def there(dx, dy, f):
        flip = 1 - core if f else core
        return lax.rem(x + dx + GX, GX), 2 * lax.rem(yc + dy + YC, YC) + flip

    def dev(dx, dy, f):
        return (*there(dx, dy, f), z)

    def hops(dx, dy):
        return min(dx, GX - dx) + min(dy, YC - dy)

    offsets = [(dx, dy, f) for dx in range(GX) for dy in range(YC) for f in range(2) if dx or dy or f]
    ring = [sorted((o for o in offsets if hops(*o[:2]) == n), key=lambda o: o[2]) for n in range(5)]
    near, two, far = ring[1] + ring[0], ring[2], ring[4] + ring[3]
    sides = [dev(1, 0, 0), dev(3, 0, 0), dev(0, 1, 0), dev(0, 3, 0)]
    corners = [dev(1, 1, 0), dev(3, 3, 0)]
    barrier = pltpu.get_barrier_semaphore()
    for o in near:
        pl.semaphore_signal(barrier, inc=1, device_id=dev(*o), device_id_type=MESH)
    perm[...] = swap16()

    for j in range(16):
        cols = slice(j * 256, (j + 1) * 256)
        t[:, cols] = jnp.dot(factor_t[...], xs[:, cols], preferred_element_type=jnp.float32).astype(jnp.bfloat16)
    for r0 in range(0, 128, 16):
        halves = [
            jnp.concatenate([t[r0:r0 + 16, h + j * 128:h + (j + 1) * 128] for j in range(16)], axis=0) for h in (0, 2048)
        ]
        block = jnp.concatenate(halves, axis=1)
        rows = jnp.dot(perm[...], block, preferred_element_type=jnp.float32).astype(jnp.bfloat16)
        buf[r0:r0 + 16] = rows.reshape(16, 16, 256)
    pl.semaphore_wait(barrier, len(near))
    for side in sides:
        pl.semaphore_signal(ready.at[0], inc=1, device_id=side, device_id_type=MESH)

    def place(px, py):
        return out.at[:, pl.ds(pl.multiple_of(py * 64 + px * 16, 16), 16), :]

    def number(dx, dy, f):
        return (dx * YC + dy) * 2 + f

    copies = []

    def push(o):
        px, py = there(*o)
        src = buf.at[pl.ds(px * 32 + py * 4, 4)]
        copies.append(remote(src, place(x, y), send.at[number(*o)], recv.at[number(*o)], dev(*o)))
        copies[-1].start()

    for o in near:
        push(o)
    pl.semaphore_wait(ready.at[0], len(sides))
    for corner in corners:
        pl.semaphore_signal(ready.at[1], inc=1, device_id=corner, device_id_type=MESH)
    for o in two:
        push(o)
    pl.semaphore_wait(ready.at[1], len(corners))
    for o in far:
        push(o)
    mine = pltpu.make_async_copy(buf.at[pl.ds(x * 32 + y * 4, 4)], place(x, y), own_sem)
    mine.start()
    for c in copies:
        c.wait_send()
    for dx, dy, f in near + two + far:
        at = place(*there(-dx, -dy, f))
        n = number(dx, dy, f)
        remote(at, at, send.at[n], recv.at[n], dev(dx, dy, f)).wait_recv()
    mine.wait()


def split3(q):
    a = q.astype(jnp.bfloat16).astype(jnp.float32)
    b = (q - a).astype(jnp.bfloat16).astype(jnp.float32)
    return a, b, q - a - b


def total_of(terms):
    while len(terms) > 1:
        terms = [terms[i] + terms[i + 1] if i + 1 < len(terms) else terms[i] for i in range(0, len(terms), 2)]
    return terms[0]


def inverse_cholesky(a, d):
    lane = lax.broadcasted_iota(jnp.int32, (8, 128), 1)
    sub = lax.broadcasted_iota(jnp.int32, (8, 128), 0)

    def repeat(v, l):
        return jnp.broadcast_to(v[:, l:l + 1], (8, 128))

    rows = [jnp.broadcast_to(a[i:i + 1, :], (8, 128)) for i in range(8)]
    for base in range(0, 128, 8):
        inside = (lane >= base) & (lane < base + 8)
        s = [[repeat(rows[i], base + k) for k in range(i + 1)] for i in range(8)]
        w = [jnp.where(inside, jnp.where(lane == base + i, 1.0, 0.0), rows[i]) for i in range(8)]
        inverse = []
        for k in range(8):
            inverse.append(1.0 / s[k][k])
            for i in range(k + 1, 8):
                m = s[i][k] * inverse[k]
                for l in range(k + 1, i + 1):
                    s[i][l] = s[i][l] - m * s[l][k]
                w[i] = w[i] - m * w[k]
        p, scale, pivot = w[0], inverse[0], s[0][0]
        for i in range(1, 8):
            p = jnp.where(sub == i, w[i], p)
            scale = jnp.where(sub == i, inverse[i], scale)
            pivot = jnp.where(sub == i, s[i][i], pivot)
        a[base:base + 8, :] = p
        d[base:base + 8, :] = pivot
        now, after = base + 8, base + 16
        if now < 128:
            before = [jnp.broadcast_to(a[now + i:now + i + 1, :], (8, 128)) for i in range(8)]
            rows = [
                jnp.where(inside, 0.0, before[i])
                - total_of([repeat(w[k], now + i) * inverse[k] * w[k] for k in range(8)])
                for i in range(8)
            ]
        if after < 128:
            u, v = split3(p), split3(p * scale)
            left = jnp.concatenate([u[0], u[0], u[1], u[0], u[1], u[2]], axis=0).astype(jnp.bfloat16)
            right = jnp.concatenate([v[0], v[1], v[0], v[2], v[1], v[0]], axis=0).astype(jnp.bfloat16)
            change = lax.dot_general(left, right, (((0,), (0,)), ((), ())), preferred_element_type=jnp.float32)
            old = a[after:, :]
            a[after:, :] = jnp.where(jnp.broadcast_to(inside[:1], old.shape), 0.0, old) - change[after:, :]


def exact_dot(u, v, dims=((1,), (0,))):
    return lax.dot_general(u, v, (dims, ((), ())), precision=lax.Precision.HIGHEST, preferred_element_type=jnp.float32)


def factor_kernel(packed, sketch, basis, factor_t, gram, image, a, d, diagonal):
    row = lax.broadcasted_iota(jnp.int32, (128, 128), 0)
    col = lax.broadcasted_iota(jnp.int32, (128, 128), 1)

    def put(r, c, block):
        gram[128 * r:128 * r + 128, 128 * c:128 * c + 128] = block
        if r < c:
            gram[128 * c:128 * c + 128, 128 * r:128 * r + 128] = block.T

    for c in range(3):
        for r in range(c + 1):
            put(r, c, packed[FIRST[c] + 128 * r:FIRST[c] + 128 * r + 128, :])
    third = packed[FIRST[3]:FIRST[3] + 224, :]
    third = jnp.concatenate([third[:, :64], third[:, 64:], jnp.zeros((64, 64), jnp.float32)], axis=0)
    fourth = packed[FIRST[4]:FIRST[4] + 256, :]
    fourth = jnp.concatenate([fourth[:, :64], fourth[:, 64:]], axis=0)
    panel = jnp.concatenate([third, fourth], axis=1)
    for r in range(3):
        put(r, 3, panel[128 * r:128 * r + 128, :])
    corner = panel[384:512, :]
    put(3, 3, jnp.where((row >= 64) & (col < 64), corner.T, corner))
    start = jnp.concatenate([sketch[at:at + n, :] for at, _, n in ORDER], axis=0).T
    def orthonormalize():
        inner = exact_dot(image[...], image[...], ((1,), (1,)))
        a[...] = inner
        diagonal[...] = jnp.where(row == col, inner, 0.0)
        inverse_cholesky(a, d)
        lower = jnp.where(col <= row, a[...] * lax.rsqrt(d[...]), 0.0)
        basis[...] = exact_dot(lower, image[...])

    def finish():
        factor_t[...] = basis[...].astype(jnp.bfloat16)

    first = exact_dot(start, gram[...])
    first = first * lax.rsqrt(jnp.sum(first * first, axis=1, keepdims=True))
    image[...] = exact_dot(first, gram[...])
    orthonormalize()
    finish()
    kept = jnp.where(row == col, d[...], 1.0) >= 1e-3 * diagonal[...]
    small = jnp.sum(jnp.where(kept, 0.0, 1.0))

    @pl.when(small > 0.0)
    def _():
        basis[...] = start

        def sweep(step, carry):
            image[...] = exact_dot(basis[...], gram[...])
            orthonormalize()
            return carry

        lax.fori_loop(0, ITERS, sweep, 0)
        finish()


def store_kernel(core, basis, out, factor, rows, sem):
    copies = [pltpu.make_async_copy(core.at[r], out.at[r], sem.at[r]) for r in range(core.shape[0])]
    for c in copies:
        c.start()
    for c in range(4):
        final = basis[:, 128 * c:128 * c + 128].T
        for at, place, n in ORDER:
            if place // 128 == c:
                rows[at:at + n, :] = final[place - 128 * c:place - 128 * c + n, :]
    copies.append(pltpu.make_async_copy(rows, factor, sem.at[4]))
    copies[-1].start()
    for c in copies:
        c.wait()


VMEM = pl.BlockSpec(memory_space=pltpu.VMEM)
ANY = pl.BlockSpec(memory_space=pl.ANY)
DMA = pltpu.SemaphoreType.DMA


def shards(field, sketch):
    xs, packed = pl.pallas_call(
        gram_kernel,
        out_shape=(
            jax.ShapeDtypeStruct((512, 4096), jnp.bfloat16),
            jax.ShapeDtypeStruct((1280, 128), jnp.float32),
        ),
        in_specs=[pl.BlockSpec(memory_space=pltpu.HBM)],
        out_specs=(VMEM, VMEM),
        scratch_shapes=[
            pltpu.VMEM((GX, 128, 16, 256), jnp.bfloat16),
            pltpu.VMEM((256, 256), jnp.bfloat16),
            pltpu.VMEM((1280, 128), jnp.float32),
            pltpu.VMEM((640, 128), jnp.float32),
            pltpu.VMEM((640, 128), jnp.float32),
            pltpu.VMEM((PLANE, 24, 128), jnp.float32),
            pltpu.VMEM((PLANE, 16, 128), jnp.float32),
            pltpu.VMEM((GZ, 24, 128), jnp.float32),
            pltpu.VMEM((GZ, 16, 128), jnp.float32),
            DMA((GX * len(PARTS),)), DMA((GX * len(PARTS),)), DMA,
            DMA((2,)), DMA((2,)),
            DMA((2, PLANE)), DMA((2, PLANE)),
            DMA((2, GZ)), DMA((2, GZ)),
            DMA((2, PLANE)), DMA((2, PLANE)),
            DMA((2, GX)), DMA((2, GX)),
        ],
        compiler_params=pltpu.CompilerParams(
            collective_id=0, has_side_effects=True, vmem_limit_bytes=24 * 2**20
        ),
        name="gram",
    )(pltpu.with_memory_space_constraint(field, pltpu.HBM))
    basis, factor_t = pl.pallas_call(
        factor_kernel,
        out_shape=(
            jax.ShapeDtypeStruct((128, 512), jnp.float32),
            jax.ShapeDtypeStruct((128, 512), jnp.bfloat16),
        ),
        in_specs=[VMEM, VMEM],
        out_specs=(VMEM, VMEM),
        scratch_shapes=[
            pltpu.VMEM((512, 512), jnp.float32),
            pltpu.VMEM((128, 512), jnp.float32),
            pltpu.VMEM((128, 128), jnp.float32),
            pltpu.VMEM((128, 128), jnp.float32),
            pltpu.VMEM((128, 128), jnp.float32),
        ],
        compiler_params=pltpu.CompilerParams(vmem_limit_bytes=16 * 2**20),
        name="factor",
    )(packed, sketch)
    core = pl.pallas_call(
        core_kernel,
        out_shape=jax.ShapeDtypeStruct((4, 512, 256), jnp.bfloat16),
        in_specs=[VMEM, VMEM],
        out_specs=VMEM,
        scratch_shapes=[
            pltpu.VMEM((256, 256), jnp.bfloat16),
            pltpu.VMEM((128, 4096), jnp.bfloat16),
            pltpu.VMEM((128, 16, 256), jnp.bfloat16),
            DMA((GX * GY,)), DMA((GX * GY,)), DMA,
            pltpu.SemaphoreType.REGULAR((2,)),
        ],
        compiler_params=pltpu.CompilerParams(
            collective_id=1, has_side_effects=True, vmem_limit_bytes=20 * 2**20
        ),
        name="core",
    )(factor_t, xs)
    core, factor = pl.pallas_call(
        store_kernel,
        out_shape=(
            jax.ShapeDtypeStruct((4, 512, 256), jnp.bfloat16),
            jax.ShapeDtypeStruct((512, 128), jnp.float32),
        ),
        in_specs=[VMEM, VMEM],
        out_specs=(ANY, ANY),
        scratch_shapes=[pltpu.VMEM((512, 128), jnp.float32), DMA((5,))],
        compiler_params=pltpu.CompilerParams(vmem_limit_bytes=16 * 2**20),
        name="store",
    )(core, basis)
    return (factor, core)


def solution(mesh):
    return jax.shard_map(
        shards,
        mesh=mesh,
        in_specs=(P("gx", "gy", "gz"), P()),
        out_specs=(P(), P(("gx", "gy"), None, "gz")),
        check_vma=False,
    )
```
